256 devices in a mesh: rows: 256 (over y, z, x, core).
Axes of the slice: x: 4, y: 4, z: 8, core: 2. Of those that a mesh axis runs over, the one named last changes fastest.
Arguments:
- features: bfloat16 [131072, 4096], P('rows'), may hold values from -90 to 90
- sketch_matrix: bfloat16 [4096, 320], replicated, may hold values from -8 to 8
Outputs:
- whitened: float32 [131072, 320], P('rows')
The draws below stay inside these ranges and needn't reach their ends.
All inputs are finite; a program needn't handle non-finite values.
Results may differ from the reference program's by a relative error of at most 0.0015.
The reference program's roundings to bfloat16 on the way count: a program that leaves them out, or rounds other values in their place, can miss the bound.
Values may be sent and summed in bfloat16 or wider, within the bound.
No kernel may reach another device: no remote copies, remote signals or barrier semaphores. Data moves between devices by JAX's collectives and lax.ppermute only.
A program may use at most 64 MiB of HBM per device.

```python
import math
import jax
import jax.numpy as jnp
from jax import lax

D = 4096
SKETCH = 320
ROWS = 131072


def draw_features(key, part):
    key = jax.random.fold_in(key, 11)
    noise_key, scale_key = jax.random.split(key)
    position = jnp.arange(ROWS, dtype=jnp.float32)[:, None] / max(ROWS - 1, 1)
    column_scale = jnp.exp(jax.random.uniform(scale_key, (1, D), jnp.float32, math.log(0.5), math.log(5.0)))
    noise = jnp.clip(jax.random.normal(noise_key, (ROWS, D), jnp.float32), -6.0, 6.0)
    rising = 1.0 + 2.0 * position
    return (noise * rising * column_scale).astype(jnp.bfloat16)


def draw_sketch_matrix(key, part):
    key = jax.random.fold_in(key, 23)
    base_key, shared_key = jax.random.split(key)
    shared = jax.random.uniform(shared_key, (D, 1), jnp.float32, -1.0, 1.0)
    base = jnp.clip(jax.random.normal(base_key, (D, SKETCH), jnp.float32), -6.0, 6.0)
    return (base + 1.5 * shared).astype(jnp.bfloat16)


def setup_inputs(seed: int = 0) -> dict:
    key_list = jax.random.split(jax.random.key(seed), 3)
    return {
        "features": draw_features(jax.random.fold_in(key_list[2], 71), 0),
        "sketch_matrix": draw_sketch_matrix(jax.random.fold_in(key_list[2], 71), 0),
    }


def gram(block):
    return jnp.einsum('rk,rl->kl', block.astype(jnp.float32), block.astype(jnp.float32), precision=lax.Precision.HIGHEST, preferred_element_type=jnp.float32)

def upper_inverse(matrix):
    lower = jnp.linalg.cholesky(matrix)
    identity = jnp.eye(matrix.shape[0], dtype=matrix.dtype)
    return lax.linalg.triangular_solve(lower, identity, left_side=True, lower=True).T

def coupling_inverse(matrix):
    upper_inv = upper_inverse(matrix)
    return jnp.dot(upper_inv, upper_inv.T, precision=lax.Precision.HIGHEST)

def reference(features, sketch_matrix):
    sketch = jnp.dot(features.astype(jnp.float32), sketch_matrix.astype(jnp.float32), preferred_element_type=jnp.float32)
    basis = jnp.dot(sketch, upper_inverse(gram(sketch)), precision=lax.Precision.HIGHEST).astype(jnp.bfloat16)
    coeffs = jnp.einsum('rd,rl->dl', features.astype(jnp.float32), basis.astype(jnp.float32), preferred_element_type=jnp.float32)
    coupling = gram(coeffs)
    projected = jnp.dot(features.astype(jnp.float32), coeffs.astype(jnp.bfloat16).astype(jnp.float32), preferred_element_type=jnp.float32)
    whitened = jnp.dot(projected, coupling_inverse(coupling), precision=lax.Precision.HIGHEST)
    return whitened * math.sqrt(ROWS)
```

```python
import functools
import math

import jax
import jax.numpy as jnp
from jax import lax
from jax.experimental import pallas as pl
from jax.experimental.pallas import tpu as pltpu
from jax.sharding import PartitionSpec as P

SKETCH = 320
PAD = 384
BLOCK = 64
LANES = 128
WIDTH = 4 * LANES
F32 = jnp.float32
BF16 = jnp.bfloat16
HIGHEST = lax.Precision.HIGHEST

FIRST_AXIS = ("x", "y")
SECOND_AXIS = ("y", "x")
STREAM_BITS = ((0, 1), (1, 0))


def coordinates(index):
    return {"c": index & 1, "x": (index >> 1) & 3, "z": (index >> 3) & 7, "y": (index >> 6) & 3}


def device_at(place):
    return ((place["y"] * 8 + place["z"]) * 4 + place["x"]) * 2 + place["c"]


def gray(value):
    return value ^ (value >> 1)


def across(block):
    return lax.ppermute(block, "rows", [(i, i ^ 1) for i in range(lax.axis_size("rows"))])


def exchange(block, stream, step):
    pairs = []
    for i in range(lax.axis_size("rows")):
        place = coordinates(i)
        axis = FIRST_AXIS[place["c"]]
        wanted = gray(place[axis]) ^ (1 << STREAM_BITS[stream][step])
        place[axis] = next(v for v in range(4) if gray(v) == wanted)
        pairs.append((i, device_at(place)))
    return lax.ppermute(block, "rows", pairs)


def all_to_all(block, axes):
    size = block.shape[0]
    groups = []
    for i in range(lax.axis_size("rows")):
        place = coordinates(i)
        axis = axes[place["c"]]
        if place[axis] == 0:
            groups.append([device_at({**place, axis: k}) for k in range(size)])
    return lax.all_to_all(block, "rows", 0, 0, axis_index_groups=groups, tiled=True)


def scatter_sum(block, axes):
    return jnp.sum(all_to_all(block, axes), axis=0)


def gather(block, axes, size):
    return all_to_all(jnp.broadcast_to(block[None], (size, *block.shape)), axes)


def order(place, half, stream):
    core = place["c"] ^ half
    code = jnp.where(core == 0, *(gray(place[axis]) for axis in FIRST_AXIS))
    first, second = STREAM_BITS[stream]
    return core, (((code >> first) & 1) << 2) | (((code >> second) & 1) << 1)


def cross_blocks(id_ref, features, sketches, outs):
    place = coordinates(id_ref[0])
    for (half, stream, start), out in outs:
        core, mask = order(place, half, stream)
        for pair in range(out.shape[0] // 2):
            there = (core << 4) | (stream << 3) | ((start + 2 * pair) ^ mask)
            columns = features[:, pl.ds(pl.multiple_of(there * LANES, 256), 256)]
            both = jnp.dot(sketches[...], columns, preferred_element_type=F32)
            cross = both[:SKETCH] + both[SKETCH:]
            out[2 * pair] = cross[:, :LANES]
            out[2 * pair + 1] = cross[:, LANES:]


def send_kernel(id_ref, features_hbm, matrix_hbm, sketches, send0, send1, features, matrix, sems):
    chunks = sems.shape[1]
    width = features.shape[1] // chunks
    copies = []
    for n in range(chunks):
        columns = slice(n * width, (n + 1) * width)
        pair = [
            pltpu.make_async_copy(source.at[:, columns], target.at[:, columns], sems.at[m, n])
            for m, (source, target) in enumerate(((matrix_hbm, matrix), (features_hbm, features)))
        ]
        for copy in pair:
            copy.start()
        copies.append((columns, pair))
    sketch_t = jnp.zeros((SKETCH, features.shape[0]), F32)
    for columns, pair in copies:
        for copy in pair:
            copy.wait()
        sketch_t += dot_nt(matrix[:, columns], features[:, columns])
    high, low = split(sketch_t, 2)
    sketches[:SKETCH, :] = high
    sketches[SKETCH:, :] = low
    cross_blocks(id_ref, features, sketches, (((1, 0, 0), send0), ((1, 1, 0), send1)))


def keep_kernel(id_ref, features, sketches, low0, high0, low1, high1):
    wanted = ((0, 0, 0), (0, 0, 4), (0, 1, 0), (0, 1, 4))
    cross_blocks(id_ref, features, sketches, tuple(zip(wanted, (low0, high0, low1, high1))))


def call(kernel, operands, outs, scratch=(), flops=0, limit=24, space=pltpu.VMEM):
    vmem = pl.BlockSpec(memory_space=pltpu.VMEM)
    return pl.pallas_call(
        kernel,
        out_shape=[jax.ShapeDtypeStruct(shape, dtype) for shape, dtype in outs],
        in_specs=[pl.BlockSpec(memory_space=pltpu.SMEM)]
        + [pl.BlockSpec(memory_space=space)] * (len(operands) - 1),
        out_specs=[vmem] * len(outs),
        scratch_shapes=scratch,
        compiler_params=pltpu.CompilerParams(vmem_limit_bytes=limit * 1024 * 1024),
        cost_estimate=pl.CostEstimate(flops=flops, bytes_accessed=4 * 1024 * 1024, transcendentals=0),
    )(*operands)


def scatter_stream(stream, low, high, received):
    back = exchange(high + received[4:], stream, 0)
    block = low + received[:4]
    back_next = exchange(block[2:] + back[2:], stream, 1)
    return block[:2] + back[:2] + back_next


def split(value, terms):
    parts = []
    for _ in range(terms):
        part = value.astype(BF16)
        parts.append(part)
        value = value - part.astype(F32)
    return parts


def dot_nt(a, b, precision=None):
    return lax.dot_general(
        a, b, (((1,), (1,)), ((), ())), precision=precision, preferred_element_type=F32
    )


def dot(a, b, precision=None):
    return jnp.dot(a, b, precision=precision, preferred_element_type=F32)


def dot_three(a, b):
    a0, a1 = split(a, 2)
    b0, b1 = split(b, 2)
    return dot(a0, b0) + (dot(a0, b1) + dot(a1, b0))


def factor_blocks(blocks, outs):
    groups = BLOCK // 8
    lane = lax.broadcasted_iota(jnp.int32, (8, LANES), 1)
    sub = lax.broadcasted_iota(jnp.int32, (8, LANES), 0)
    work = []
    for block in blocks:
        rows = []
        for g in range(groups):
            unit = jnp.where(lane - BLOCK == sub + 8 * g, 1.0, 0.0).astype(F32)
            rows.append(jnp.where(lane < BLOCK, block[8 * g : 8 * g + 8], unit))
        work.append(rows)
    for g in range(groups):
        columns = [
            [
                [
                    jnp.broadcast_to(rows[r][:, 8 * g + j : 8 * g + j + 1], (8, LANES))
                    for r in range(g, groups)
                ]
                for j in range(8)
            ]
            for rows in work
        ]
        for k in range(8):
            for rows, cols, out in zip(work, columns, outs):
                pivot = cols[k][0][k : k + 1, :]
                inverse = 1.0 / pivot
                row = rows[g][k : k + 1, :]
                out[8 * g + k : 8 * g + k + 1, :] = row * lax.rsqrt(pivot)
                scaled = row * inverse
                for j in range(k + 1, 8):
                    factor = cols[j][0][k : k + 1, :] * inverse
                    for r in range(groups - g):
                        cols[j][r] = cols[j][r] - cols[k][r] * factor
                for r in range(g, groups):
                    column = cols[k][r - g]
                    if r == g:
                        column = jnp.where(sub > k, column, 0.0)
                    rows[r] = rows[r] - column * scaled


def factor_all(mats, outs, upper):
    column = lax.broadcasted_iota(jnp.int32, (BLOCK, PAD), 1)
    row = lax.broadcasted_iota(jnp.int32, (BLOCK, PAD), 0)
    lane = lax.broadcasted_iota(jnp.int32, (BLOCK, LANES), 1)
    line = lax.broadcasted_iota(jnp.int32, (BLOCK, LANES), 0)
    steps = SKETCH // BLOCK
    for step in range(steps):
        here = slice(step * BLOCK, (step + 1) * BLOCK)
        window = slice(step // 2 * LANES, (step // 2 + 1) * LANES)
        odd = step % 2 == 1
        blocks = []
        for mat in mats:
            block = mat[here, window]
            blocks.append(pltpu.roll(block, BLOCK, 1) if odd else block)
        factor_blocks(blocks, outs)
        inside = (column >= step * BLOCK) & (column < (step + 1) * BLOCK)
        for n, (mat, out) in enumerate(zip(mats, outs)):
            both = out[...]
            inverse = pltpu.roll(both, BLOCK, 1)[:, :BLOCK]
            line_up = jnp.where(inside, jnp.where(column - step * BLOCK == row, 1.0, 0.0), mat[here, :])
            panel = dot(inverse, line_up, HIGHEST)
            mat[here, :] = panel
            if n == 0:
                upper[here, :] = jnp.where(column >= (step + 1) * BLOCK, panel, 0.0)
                corner = jnp.where((lane < BLOCK) & (lane >= line), both, 0.0)
                corner = pltpu.roll(corner, BLOCK, 1) if odd else corner
                upper[here, window] = upper[here, window] + corner
            if step < steps - 1:
                start = (step + 1) * BLOCK // LANES * LANES
                change = dot(jnp.transpose(panel[:, start:]), panel, HIGHEST)
                below = slice((step + 1) * BLOCK, SKETCH)
                skip = (step + 1) * BLOCK - start
                keep = lax.broadcasted_iota(jnp.int32, (SKETCH - (step + 1) * BLOCK, PAD), 1)
                keep = (keep < step * BLOCK) | (keep >= (step + 1) * BLOCK)
                mat[below, :] = (
                    jnp.where(keep, mat[below, :], 0.0)
                    - change[skip : skip + SKETCH - (step + 1) * BLOCK]
                )


def columns_of(place, half, part, stream):
    core, mask = order(place, half, stream)
    first = (core << 4) | (stream << 3) | ((4 * part) ^ (mask & 4))
    return pl.ds(pl.multiple_of(first * LANES, WIDTH), WIDTH)


def lay_out(place, members, pieces, cross):
    for n, ((half, part, stream), piece) in enumerate(zip(members, pieces)):
        if len(piece.shape) == 2:
            cross[:, n * WIDTH : (n + 1) * WIDTH] = piece[...]
            continue
        _, mask = order(place, half, stream)
        for slot in range(4):
            start = n * WIDTH + (slot ^ (mask & 2)) * LANES
            cross[:, pl.ds(pl.multiple_of(start, LANES), LANES)] = piece[slot]


def products(place, members, cross, sketch_matrix_t, gram, coupling, left, right, mix):
    a, b, c = split(cross[...], 3)
    for n, term in enumerate((a, b, c)):
        left[n * SKETCH : (n + 1) * SKETCH, :] = term
    right[:SKETCH, :] = a
    right[SKETCH:PAD, :] = jnp.zeros((PAD - SKETCH, a.shape[1]), BF16)
    for n, member in enumerate(members):
        right[PAD:, n * WIDTH : (n + 1) * WIDTH] = sketch_matrix_t[:, columns_of(place, *member)]
    both = dot_nt(left[...], right[...])
    terms = [both[n * SKETCH : (n + 1) * SKETCH] for n in range(3)]
    for ref in (gram, coupling, mix):
        ref[...] = jnp.zeros_like(ref)
    gram[:SKETCH, :SKETCH] = terms[0][:, PAD:] + (terms[1][:, PAD:] + terms[2][:, PAD:])
    mix[:SKETCH, :SKETCH] = terms[1][:, :SKETCH] + terms[2][:, :SKETCH]
    coupling[:SKETCH, :SKETCH] = terms[0][:, :SKETCH] + dot_nt(b, b)
    coupling[...] += mix[...] + jnp.transpose(mix[...])


def pieces_kernel(members, id_ref, sketch_matrix_t, *refs):
    pieces, (cross, *rest) = refs[: len(members)], refs[len(members) :]
    place = coordinates(id_ref[0])
    lay_out(place, members, pieces, cross)
    products(place, members, cross, sketch_matrix_t, *rest)


def factor_kernel(members, scale, id_ref, sketch_matrix_t, *refs):
    pieces, refs = refs[: len(members)], refs[len(members) :]
    sums, (cross, basis_map, inverse_c) = refs[:6], refs[6:9]
    gram, coupling, left, right, mix, upper, out0, out1, wide = refs[9:]
    place = coordinates(id_ref[0])
    lay_out(place, members, pieces, cross)
    products(place, members, cross, sketch_matrix_t, gram, coupling, left, right, mix)
    gram[...] += sums[0][...] + (sums[2][...] + sums[4][...])
    coupling[...] += sums[1][...] + (sums[3][...] + sums[5][...])
    upper[...] = jnp.zeros_like(upper)
    factor_all((gram, coupling), (out0, out1), upper)
    row = lax.broadcasted_iota(jnp.int32, (PAD, PAD), 0)
    column = lax.broadcasted_iota(jnp.int32, (PAD, PAD), 1)
    lower = (row < SKETCH) & (column <= row)
    high, low = split(jnp.where(lower, gram[...], 0.0)[:SKETCH, :SKETCH], 2)
    for n, term in enumerate((high, high, low)):
        wide[:, n * SKETCH : (n + 1) * SKETCH] = term.astype(F32)
    basis_map[...] = wide[...].astype(BF16)
    chain = dot_nt(jnp.where(lower, coupling[...], 0.0), upper[...], HIGHEST)
    mix[...] = dot(jnp.transpose(chain), chain, HIGHEST) * scale
    inverse_c[...] = mix[:SKETCH, :SKETCH]


def final_kernel(sets, id_ref, features, basis_map, inverse_c, *refs):
    crosses, (result, stack) = refs[:-2], refs[-2:]
    place = coordinates(id_ref[0])
    total = jnp.zeros(result.shape, F32)
    for cross, members in zip(crosses, sets):
        for n, member in enumerate(members):
            a, b = split(cross[:, n * WIDTH : (n + 1) * WIDTH], 2)
            for m, term in enumerate((a, b, a)):
                stack[m * SKETCH : (m + 1) * SKETCH, :] = term
            coeffs = dot(basis_map[...], stack[...])
            total += dot_nt(coeffs.astype(BF16), features[:, columns_of(place, *member)])
    result[...] = dot_three(inverse_c[...], total)


def body(features, sketch_matrix):
    rows, width = features.shape
    rows_total = rows * lax.axis_size("rows")
    device = lax.axis_index("rows").astype(jnp.int32)[None]
    whole, piece = ((8, SKETCH, LANES), F32), ((4, SKETCH, LANES), F32)
    flops = 2 * rows * width * SKETCH

    sketch_matrix_t = sketch_matrix.T

    sketches, send0, send1 = call(
        send_kernel,
        (device, features, sketch_matrix_t),
        [((2 * SKETCH, rows), BF16), whole, whole],
        scratch=[
            pltpu.VMEM((rows, width), BF16),
            pltpu.VMEM((SKETCH, width), BF16),
            pltpu.SemaphoreType.DMA((2, 4)),
        ],
        flops=2 * flops,
        space=pltpu.HBM,
        limit=50,
    )
    received = across(send0), across(send1)
    low0, high0, low1, high1 = call(
        keep_kernel, (device, features, sketches), [piece] * 4, flops=flops
    )
    block = jnp.concatenate(
        [scatter_stream(0, low0, high0, received[0]), scatter_stream(1, low1, high1, received[1])]
    )
    block = scatter_sum(block, SECOND_AXIS)
    block = scatter_sum(block.reshape(8, SKETCH // 8, LANES), ("z", "z"))
    block = gather(block, ("z", "z"), 8).reshape(SKETCH, LANES)
    block = gather(block, SECOND_AXIS, 4)
    first, second = [], []
    for stream in range(2):
        own = block[2 * stream : 2 * stream + 2]
        own = jnp.concatenate([own, exchange(own, stream, 1)])
        first.append(own)
        second.append(exchange(own, stream, 0))

    sets = [
        ((0, 0, 0),),
        ((0, 0, 1), (0, 1, 0), (0, 1, 1)),
        ((1, 0, 0), (1, 0, 1)),
        ((1, 1, 0), (1, 1, 1)),
    ]
    square = ((PAD, PAD), F32)

    def scratch_for(members):
        width = len(members) * WIDTH
        return [
            pltpu.VMEM((3 * SKETCH, width), BF16),
            pltpu.VMEM((PAD + SKETCH, width), BF16),
            pltpu.VMEM(*square),
        ]

    def cross_shape(members):
        return ((SKETCH, len(members) * WIDTH), F32)

    def sums_of(members, pieces):
        return call(
            functools.partial(pieces_kernel, members),
            (device, sketch_matrix_t, *pieces),
            [cross_shape(members), square, square],
            scratch=scratch_for(members),
        )

    cross0, *sums0 = sums_of(sets[0], first[:1])
    other = [across(block) for block in (cross0, first[1], *second)]
    cross1, *sums1 = sums_of(sets[1], [first[1], *second])
    cross2, *sums2 = sums_of(sets[2], other[:2])
    corner = pltpu.VMEM((BLOCK, LANES), F32)
    cross3, basis_map, inverse_c = call(
        functools.partial(factor_kernel, sets[3], math.sqrt(rows_total)),
        (device, sketch_matrix_t, *other[2:], *sums0, *sums1, *sums2),
        [cross_shape(sets[3]), ((SKETCH, 3 * SKETCH), BF16), ((SKETCH, SKETCH), F32)],
        scratch=[pltpu.VMEM(*square)] * 2
        + scratch_for(sets[3])
        + [pltpu.VMEM(*square), corner, corner, pltpu.VMEM((SKETCH, 3 * SKETCH), F32)],
        flops=flops,
    )
    (result,) = call(
        functools.partial(final_kernel, sets),
        (device, features, basis_map, inverse_c, cross0, cross1, cross2, cross3),
        [((SKETCH, rows), F32)],
        scratch=[pltpu.VMEM((3 * SKETCH, WIDTH), BF16)],
        flops=4 * flops,
    )
    return result.T


def solution(mesh):
    return jax.shard_map(
        body,
        mesh=mesh,
        in_specs=(P("rows", None), P()),
        out_specs=P("rows", None),
        check_vma=False,
    )
```

```python
import functools
import math

import jax
import jax.numpy as jnp
from jax import lax
from jax.experimental import pallas as pl
from jax.experimental.pallas import tpu as pltpu
from jax.sharding import PartitionSpec as P

SKETCH = 320
PAD = 384
BLOCK = 64
LANES = 128
WIDTH = 4 * LANES
F32 = jnp.float32
BF16 = jnp.bfloat16

FIRST_AXIS = ("y", "x")
SECOND_AXIS = ("x", "y")
STREAM_BITS = ((0, 1), (1, 0))


def coordinates(index):
    return {"c": index & 1, "x": (index >> 1) & 3, "z": (index >> 3) & 7, "y": (index >> 6) & 3}


def device_at(place):
    return ((place["y"] * 8 + place["z"]) * 4 + place["x"]) * 2 + place["c"]


def gray(value):
    return value ^ (value >> 1)


def across(block):
    return lax.ppermute(block, "rows", [(i, i ^ 1) for i in range(lax.axis_size("rows"))])


def exchange(block, stream, step):
    pairs = []
    for i in range(lax.axis_size("rows")):
        place = coordinates(i)
        axis = FIRST_AXIS[place["c"]]
        wanted = gray(place[axis]) ^ (1 << STREAM_BITS[stream][step])
        place[axis] = next(v for v in range(4) if gray(v) == wanted)
        pairs.append((i, device_at(place)))
    return lax.ppermute(block, "rows", pairs)


def all_to_all(block, axes):
    size = block.shape[0]
    groups = []
    for i in range(lax.axis_size("rows")):
        place = coordinates(i)
        axis = axes[place["c"]]
        if place[axis] == 0:
            groups.append([device_at({**place, axis: k}) for k in range(size)])
    return lax.all_to_all(block, "rows", 0, 0, axis_index_groups=groups, tiled=True)


def scatter_sum(block, axes):
    return jnp.sum(all_to_all(block, axes), axis=0)


def gather(block, axes, size):
    return all_to_all(jnp.broadcast_to(block[None], (size, *block.shape)), axes)


def order(place, half, stream):
    core = place["c"] ^ half
    code = jnp.where(core == 0, *(gray(place[axis]) for axis in FIRST_AXIS))
    first, second = STREAM_BITS[stream]
    return core, (((code >> first) & 1) << 2) | (((code >> second) & 1) << 1)


def cross_blocks(id_ref, features, sketches, outs):
    place = coordinates(id_ref[0])
    for (half, stream, start), out in outs:
        core, mask = order(place, half, stream)
        for pair in range(out.shape[0] // 2):
            there = (core << 4) | (stream << 3) | ((start + 2 * pair) ^ mask)
            columns = features[:, pl.ds(pl.multiple_of(there * LANES, 256), 256)]
            both = jnp.dot(sketches[...], columns, preferred_element_type=F32)
            cross = both[:SKETCH] + both[SKETCH:]
            out[2 * pair] = cross[:, :LANES]
            out[2 * pair + 1] = cross[:, LANES:]


def send_kernel(id_ref, features_hbm, matrix_hbm, sketches, send0, send1, features, matrix, sems):
    chunks = sems.shape[1]
    width = features.shape[1] // chunks
    copies = []
    for n in range(chunks):
        columns = slice(n * width, (n + 1) * width)
        pair = [
            pltpu.make_async_copy(source.at[:, columns], target.at[:, columns], sems.at[m, n])
            for m, (source, target) in enumerate(((matrix_hbm, matrix), (features_hbm, features)))
        ]
        for copy in pair:
            copy.start()
        copies.append((columns, pair))
    sketch_t = jnp.zeros((SKETCH, features.shape[0]), F32)
    for columns, pair in copies:
        for copy in pair:
            copy.wait()
        sketch_t += dot_nt(matrix[:, columns], features[:, columns])
    high, low = split(sketch_t, 2)
    sketches[:SKETCH, :] = high
    sketches[SKETCH:, :] = low
    cross_blocks(id_ref, features, sketches, (((1, 0, 0), send0), ((1, 1, 0), send1)))


def keep_kernel(id_ref, features, sketches, low0, high0, low1, high1):
    wanted = ((0, 0, 0), (0, 0, 4), (0, 1, 0), (0, 1, 4))
    cross_blocks(id_ref, features, sketches, tuple(zip(wanted, (low0, high0, low1, high1))))


def call(kernel, operands, outs, scratch=(), flops=0, limit=24, space=pltpu.VMEM):
    vmem = pl.BlockSpec(memory_space=pltpu.VMEM)
    return pl.pallas_call(
        kernel,
        out_shape=[jax.ShapeDtypeStruct(shape, dtype) for shape, dtype in outs],
        in_specs=[pl.BlockSpec(memory_space=pltpu.SMEM)]
        + [pl.BlockSpec(memory_space=space)] * (len(operands) - 1),
        out_specs=[vmem] * len(outs),
        scratch_shapes=scratch,
        compiler_params=pltpu.CompilerParams(vmem_limit_bytes=limit * 1024 * 1024),
        cost_estimate=pl.CostEstimate(flops=flops, bytes_accessed=4 * 1024 * 1024, transcendentals=0),
    )(*operands)


def scatter_stream(stream, low, high, received):
    back = exchange(high + received[4:], stream, 0)
    block = low + received[:4]
    back_next = exchange(block[2:] + back[2:], stream, 1)
    return block[:2] + back[:2] + back_next


def split(value, terms):
    parts = []
    for _ in range(terms):
        part = value.astype(BF16)
        parts.append(part)
        value = value - part.astype(F32)
    return parts


def dot_nt(a, b, precision=None):
    return lax.dot_general(
        a, b, (((1,), (1,)), ((), ())), precision=precision, preferred_element_type=F32
    )


def dot(a, b, precision=None):
    return jnp.dot(a, b, precision=precision, preferred_element_type=F32)


def dot_three(a, b):
    a0, a1 = split(a, 2)
    b0, b1 = split(b, 2)
    return dot(a0, b0) + (dot(a0, b1) + dot(a1, b0))


def stacked(rows, terms):
    parts = split(rows, 3)
    return jnp.concatenate([parts[n] for n in terms], axis=0)


def beside(value):
    lane = lax.broadcasted_iota(jnp.int32, value.shape, 1)
    parts = [part.astype(F32) for part in split(value, 3)]
    turned = [pltpu.roll(part, BLOCK, 1) for part in parts[:2]]
    pairs = ((0, 0), (1, 0), (2, 1))
    return jnp.concatenate(
        [jnp.where(lane < BLOCK, parts[m], turned[n]).astype(BF16) for m, n in pairs], axis=1
    )


UNDER = (0, 1, 0, 2, 0, 1)


def factor_blocks(blocks, outs, meanwhile):
    groups = BLOCK // 8
    lane = lax.broadcasted_iota(jnp.int32, (8, LANES), 1)
    sub = lax.broadcasted_iota(jnp.int32, (8, LANES), 0)
    work = []
    for block in blocks:
        rows = []
        for g in range(groups):
            unit = jnp.where(lane - BLOCK == sub + 8 * g, 1.0, 0.0).astype(F32)
            rows.append(jnp.where(lane < BLOCK, block[8 * g : 8 * g + 8], unit))
        work.append(rows)
    for g in range(groups):
        columns = [
            [
                [
                    jnp.broadcast_to(rows[r][:, 8 * g + j : 8 * g + j + 1], (8, LANES))
                    for r in range(g, groups)
                ]
                for j in range(8)
            ]
            for rows in work
        ]
        for k in range(8):
            for rows, cols, out in zip(work, columns, outs):
                pivot = cols[k][0][k : k + 1, :]
                inverse = 1.0 / pivot
                row = rows[g][k : k + 1, :]
                out[8 * g + k : 8 * g + k + 1, :] = row * lax.rsqrt(pivot)
                scaled = row * inverse
                for j in range(k + 1, 8):
                    factor = cols[j][0][k : k + 1, :] * inverse
                    for r in range(groups - g):
                        cols[j][r] = cols[j][r] - cols[k][r] * factor
                for r in range(g, groups):
                    column = cols[k][r - g]
                    if r == g:
                        column = jnp.where(sub > k, column, 0.0)
                    rows[r] = rows[r] - column * scaled
        if meanwhile:
            meanwhile.pop(0)()


def factor_all(mats, outs, upper):
    column = lax.broadcasted_iota(jnp.int32, (BLOCK, PAD), 1)
    row = lax.broadcasted_iota(jnp.int32, (BLOCK, PAD), 0)
    lane = lax.broadcasted_iota(jnp.int32, (BLOCK, LANES), 1)
    line = lax.broadcasted_iota(jnp.int32, (BLOCK, LANES), 0)
    steps = SKETCH // BLOCK
    meanwhile = []

    def update(mat, change, step, first, last):
        rows = slice(first * BLOCK, last * BLOCK)
        keep = lax.broadcasted_iota(jnp.int32, ((last - first) * BLOCK, PAD), 1)
        keep = (keep < step * BLOCK) | (keep >= (step + 1) * BLOCK)
        mat[rows, :] = jnp.where(keep, mat[rows, :], 0.0) - change

    for step in range(steps):
        here = slice(step * BLOCK, (step + 1) * BLOCK)
        window = slice(step // 2 * LANES, (step // 2 + 1) * LANES)
        odd = step % 2 == 1
        blocks = []
        for mat in mats:
            block = mat[here, window]
            blocks.append(pltpu.roll(block, BLOCK, 1) if odd else block)
        factor_blocks(blocks, outs, meanwhile)
        inside = (column >= step * BLOCK) & (column < (step + 1) * BLOCK)
        for n, (mat, out) in enumerate(zip(mats, outs)):
            both = out[...]
            inverse = beside(pltpu.roll(both, BLOCK, 1))
            line_up = jnp.where(inside, jnp.where(column - step * BLOCK == row, 1.0, 0.0), mat[here, :])
            panel = dot(inverse, stacked(line_up, UNDER))
            mat[here, :] = panel
            if n == 0:
                upper[here, :] = jnp.where(column >= (step + 1) * BLOCK, panel, 0.0)
                corner = jnp.where((lane < BLOCK) & (lane >= line), both, 0.0)
                corner = pltpu.roll(corner, BLOCK, 1) if odd else corner
                upper[here, window] = upper[here, window] + corner
            if step == steps - 1:
                continue
            start = (step + 1) * BLOCK // LANES * LANES
            turned = jnp.transpose(panel[:, start:])
            turned = jnp.concatenate([turned, jnp.zeros_like(turned)], axis=1)
            left, right = beside(turned), stacked(panel, UNDER)
            skip = (step + 1) * BLOCK - start
            update(mat, dot(left[skip : skip + BLOCK], right), step, step + 1, step + 2)
            if step < steps - 2:

                def rest(mat=mat, left=left, right=right, step=step, skip=skip):
                    stop = SKETCH - start_of(step)
                    update(mat, dot(left[skip + BLOCK : stop], right), step, step + 2, steps)

                def start_of(step):
                    return (step + 1) * BLOCK // LANES * LANES

                meanwhile.append(rest)


def columns_of(place, half, part, stream):
    core, mask = order(place, half, stream)
    first = (core << 4) | (stream << 3) | ((4 * part) ^ (mask & 4))
    return pl.ds(pl.multiple_of(first * LANES, WIDTH), WIDTH)


def pieces_kernel(member, id_ref, sketch_matrix_t, piece, *refs):
    before, (terms, sums, left, right, cross, mix) = refs[:-6], refs[-6:]
    place = coordinates(id_ref[0])
    _, mask = order(place, member[0], member[2])
    for slot in range(4):
        start = (slot ^ (mask & 2)) * LANES
        cross[:, pl.ds(pl.multiple_of(start, LANES), LANES)] = piece[slot]
    a, b, c = split(cross[...], 3)
    for n, (term, again) in enumerate(((a, a), (b, b), (c, a))):
        left[n * SKETCH : (n + 1) * SKETCH, :] = term
        terms[n * SKETCH : (n + 1) * SKETCH, :] = again
    right[:SKETCH, :] = a
    right[SKETCH:PAD, :] = jnp.zeros((PAD - SKETCH, WIDTH), BF16)
    right[PAD:, :] = sketch_matrix_t[:, columns_of(place, *member)]
    both = dot_nt(left[...], right[...])
    parts = [both[n * SKETCH : (n + 1) * SKETCH] for n in range(3)]
    mix[...] = jnp.zeros_like(mix)
    mix[:SKETCH, :SKETCH] = parts[1][:, :SKETCH] + parts[2][:, :SKETCH]
    mixed = (mix[...] + jnp.transpose(mix[...]))[:SKETCH]
    sums[...] = before[0][...] if before else jnp.zeros_like(sums)
    sums[0, :, :SKETCH] += parts[0][:, PAD:] + (parts[1][:, PAD:] + parts[2][:, PAD:])
    sums[1, :, :SKETCH] += parts[0][:, :SKETCH] + dot_nt(b, b)
    sums[1] += mixed


def factor_kernel(scale, id_ref, own, other, basis_map, inverse_c, gram, coupling, upper, out0, out1, wide):
    for n, ref in enumerate((gram, coupling)):
        ref[...] = jnp.zeros_like(ref)
        ref[:SKETCH, :] = own[n] + other[n]
    upper[...] = jnp.zeros_like(upper)
    factor_all((gram, coupling), (out0, out1), upper)
    row = lax.broadcasted_iota(jnp.int32, (PAD, PAD), 0)
    column = lax.broadcasted_iota(jnp.int32, (PAD, PAD), 1)
    lower = (row < SKETCH) & (column <= row)
    high, low = split(jnp.where(lower, gram[...], 0.0)[:SKETCH, :SKETCH], 2)
    for n, term in enumerate((high, high, low)):
        wide[:, n * SKETCH : (n + 1) * SKETCH] = term.astype(F32)
    basis_map[...] = wide[...].astype(BF16)
    chain = dot_three(jnp.where(lower, coupling[...], 0.0), jnp.transpose(upper[...]))
    gram[...] = dot_three(jnp.transpose(chain), chain) * scale
    inverse_c[...] = gram[:SKETCH, :SKETCH]


def final_kernel(members, id_ref, features, basis_map, inverse_c, *refs):
    terms, result = refs[:-1], refs[-1]
    place = coordinates(id_ref[0])
    total = jnp.zeros(result.shape, F32)
    for term, member in zip(terms, members):
        coeffs = dot(basis_map[...], term[...])
        total += dot_nt(coeffs.astype(BF16), features[:, columns_of(place, *member)])
    result[...] = dot_three(inverse_c[...], total)


def body(features, sketch_matrix):
    rows, width = features.shape
    rows_total = rows * lax.axis_size("rows")
    device = lax.axis_index("rows").astype(jnp.int32)[None]
    whole, piece = ((8, SKETCH, LANES), F32), ((4, SKETCH, LANES), F32)
    flops = 2 * rows * width * SKETCH

    sketch_matrix_t = sketch_matrix.T

    sketches, send0, send1 = call(
        send_kernel,
        (device, features, sketch_matrix_t),
        [((2 * SKETCH, rows), BF16), whole, whole],
        scratch=[
            pltpu.VMEM((rows, width), BF16),
            pltpu.VMEM((SKETCH, width), BF16),
            pltpu.SemaphoreType.DMA((2, 4)),
        ],
        flops=2 * flops,
        space=pltpu.HBM,
        limit=50,
    )
    received = across(send0), across(send1)
    low0, high0, low1, high1 = call(
        keep_kernel, (device, features, sketches), [piece] * 4, flops=flops
    )
    block = jnp.concatenate(
        [scatter_stream(0, low0, high0, received[0]), scatter_stream(1, low1, high1, received[1])]
    )
    block = scatter_sum(block, SECOND_AXIS)
    block = scatter_sum(block.reshape(8, SKETCH // 8, LANES), ("z", "z"))
    block = gather(block, ("z", "z"), 8).reshape(SKETCH, LANES)
    block = gather(block, SECOND_AXIS, 4)
    streams = []
    for stream in range(2):
        own = block[2 * stream : 2 * stream + 2]
        own = jnp.concatenate([own, exchange(own, stream, 1)])
        streams.append((own, exchange(own, stream, 0)))

    members = [(0, part, stream) for part in range(2) for stream in range(2)]
    terms_shape = ((3 * SKETCH, WIDTH), BF16)
    sums_shape = ((2, SKETCH, PAD), F32)
    terms, sums = [], ()
    for member in members:
        _, part, stream = member
        term, *sums = call(
            functools.partial(pieces_kernel, member),
            (device, sketch_matrix_t, streams[stream][part], *sums),
            [terms_shape, sums_shape],
            scratch=[
                pltpu.VMEM(*terms_shape),
                pltpu.VMEM((PAD + SKETCH, WIDTH), BF16),
                pltpu.VMEM((SKETCH, WIDTH), F32),
                pltpu.VMEM((PAD, PAD), F32),
            ],
        )
        terms.append(term)
    square, corner = pltpu.VMEM((PAD, PAD), F32), pltpu.VMEM((BLOCK, LANES), F32)
    basis_map, inverse_c = call(
        functools.partial(factor_kernel, math.sqrt(rows_total)),
        (device, *sums, across(*sums)),
        [((SKETCH, 3 * SKETCH), BF16), ((SKETCH, SKETCH), F32)],
        scratch=[square] * 3 + [corner] * 2 + [pltpu.VMEM((SKETCH, 3 * SKETCH), F32)],
        flops=14 * flops,
    )
    terms += [across(term) for term in terms]
    members += [(1, part, stream) for _, part, stream in members]
    (result,) = call(
        functools.partial(final_kernel, members),
        (device, features, basis_map, inverse_c, *terms),
        [((SKETCH, rows), F32)],
        flops=4 * flops,
    )
    return result.T


def solution(mesh):
    return jax.shard_map(
        body,
        mesh=mesh,
        in_specs=(P("rows", None), P()),
        out_specs=P("rows", None),
        check_vma=False,
    )
```

```python
import functools
import math

import jax
import jax.numpy as jnp
from jax import lax
from jax.experimental import pallas as pl
from jax.experimental.pallas import tpu as pltpu
from jax.sharding import PartitionSpec as P

SKETCH = 320
PAD = 384
BLOCK = 64
LANES = 128
WIDTH = 4 * LANES
F32 = jnp.float32
BF16 = jnp.bfloat16

FIRST_AXIS = ("y", "x")
SECOND_AXIS = ("x", "y")
STREAM_BITS = ((0, 1), (1, 0))


def coordinates(index):
    return {"c": index & 1, "x": (index >> 1) & 3, "z": (index >> 3) & 7, "y": (index >> 6) & 3}


def device_at(place):
    return ((place["y"] * 8 + place["z"]) * 4 + place["x"]) * 2 + place["c"]


def gray(value):
    return value ^ (value >> 1)


def across(block):
    return lax.ppermute(block, "rows", [(i, i ^ 1) for i in range(lax.axis_size("rows"))])


def exchange(block, stream, step):
    pairs = []
    for i in range(lax.axis_size("rows")):
        place = coordinates(i)
        axis = FIRST_AXIS[place["c"]]
        wanted = gray(place[axis]) ^ (1 << STREAM_BITS[stream][step])
        place[axis] = next(v for v in range(4) if gray(v) == wanted)
        pairs.append((i, device_at(place)))
    return lax.ppermute(block, "rows", pairs)


def all_to_all(block):
    groups = []
    for i in range(lax.axis_size("rows")):
        place = coordinates(i)
        axis = SECOND_AXIS[place["c"]]
        if place[axis] == 0 and place["z"] == 0:
            groups.append([device_at({**place, axis: a, "z": z}) for a in range(4) for z in range(8)])
    return lax.all_to_all(block, "rows", 0, 0, axis_index_groups=groups, tiled=True)


def order(place, half, stream):
    core = place["c"] ^ half
    code = jnp.where(core == 0, *(gray(place[axis]) for axis in FIRST_AXIS))
    first, second = STREAM_BITS[stream]
    return core, (((code >> first) & 1) << 2) | (((code >> second) & 1) << 1)


def cross_blocks(id_ref, features, sketches, outs):
    place = coordinates(id_ref[0])
    for (half, stream, start), out in outs:
        core, mask = order(place, half, stream)
        for pair in range(out.shape[0] // 2):
            there = (core << 4) | (stream << 3) | ((start + 2 * pair) ^ mask)
            columns = features[:, pl.ds(pl.multiple_of(there * LANES, 256), 256)]
            both = jnp.dot(sketches[...], columns, preferred_element_type=F32)
            cross = both[:SKETCH] + both[SKETCH:]
            out[2 * pair] = cross[:, :LANES]
            out[2 * pair + 1] = cross[:, LANES:]


def send_kernel(id_ref, features_hbm, matrix_hbm, sketches, send0, send1, features, matrix, sems):
    chunks = sems.shape[0] - 1
    height = features.shape[0] // chunks
    copies = [pltpu.make_async_copy(matrix_hbm, matrix, sems.at[chunks])]
    for n in range(chunks):
        rows = slice(n * height, (n + 1) * height)
        copies.append(pltpu.make_async_copy(features_hbm.at[rows], features.at[rows], sems.at[n]))
    for copy in copies:
        copy.start()
    copies[0].wait()
    for n in range(chunks):
        copies[n + 1].wait()
        rows = slice(n * height, (n + 1) * height)
        high, low = split(dot_nt(matrix[...], features[rows, :]), 2)
        sketches[:SKETCH, rows] = high
        sketches[SKETCH:, rows] = low
    cross_blocks(id_ref, features, sketches, (((1, 0, 0), send0), ((1, 1, 0), send1)))


def keep_kernel(id_ref, features, sketches, low0, high0, low1, high1):
    wanted = ((0, 0, 0), (0, 0, 4), (0, 1, 0), (0, 1, 4))
    cross_blocks(id_ref, features, sketches, tuple(zip(wanted, (low0, high0, low1, high1))))


def call(kernel, operands, outs, scratch=(), flops=0, limit=24, space=pltpu.VMEM):
    vmem = pl.BlockSpec(memory_space=pltpu.VMEM)
    return pl.pallas_call(
        kernel,
        out_shape=[jax.ShapeDtypeStruct(shape, dtype) for shape, dtype in outs],
        in_specs=[pl.BlockSpec(memory_space=pltpu.SMEM)]
        + [pl.BlockSpec(memory_space=space)] * (len(operands) - 1),
        out_specs=[vmem] * len(outs),
        scratch_shapes=scratch,
        compiler_params=pltpu.CompilerParams(vmem_limit_bytes=limit * 1024 * 1024),
        cost_estimate=pl.CostEstimate(flops=flops, bytes_accessed=4 * 1024 * 1024, transcendentals=0),
    )(*operands)


def scatter_stream(stream, low, high, received):
    back = exchange(high + received[4:], stream, 0)
    block = low + received[:4]
    back_next = exchange(block[2:] + back[2:], stream, 1)
    return block[:2] + back[:2] + back_next


def split(value, terms):
    parts = []
    for _ in range(terms):
        part = value.astype(BF16)
        parts.append(part)
        value = value - part.astype(F32)
    return parts


def dot_nt(a, b, precision=None):
    return lax.dot_general(
        a, b, (((1,), (1,)), ((), ())), precision=precision, preferred_element_type=F32
    )


def dot(a, b, precision=None):
    return jnp.dot(a, b, precision=precision, preferred_element_type=F32)


def dot_three(a, b):
    a0, a1 = split(a, 2)
    b0, b1 = split(b, 2)
    return dot(a0, b0) + (dot(a0, b1) + dot(a1, b0))


def stacked(rows, terms):
    parts = split(rows, 3)
    return jnp.concatenate([parts[n] for n in terms], axis=0)


def beside(value):
    lane = lax.broadcasted_iota(jnp.int32, value.shape, 1)
    parts = [part.astype(F32) for part in split(value, 3)]
    turned = [pltpu.roll(part, BLOCK, 1) for part in parts[:2]]
    pairs = ((0, 0), (1, 0), (2, 1))
    return jnp.concatenate(
        [jnp.where(lane < BLOCK, parts[m], turned[n]).astype(BF16) for m, n in pairs], axis=1
    )


UNDER = (0, 1, 0, 2, 0, 1)


def factor_blocks(blocks, outs, meanwhile):
    groups = BLOCK // 8
    lane = lax.broadcasted_iota(jnp.int32, (8, LANES), 1)
    sub = lax.broadcasted_iota(jnp.int32, (8, LANES), 0)
    work = []
    for block in blocks:
        rows = []
        for g in range(groups):
            unit = jnp.where(lane - BLOCK == sub + 8 * g, 1.0, 0.0).astype(F32)
            rows.append(jnp.where(lane < BLOCK, block[8 * g : 8 * g + 8], unit))
        work.append(rows)
    for g in range(groups):
        columns = [
            [
                [
                    jnp.broadcast_to(rows[r][:, 8 * g + j : 8 * g + j + 1], (8, LANES))
                    for r in range(g, groups)
                ]
                for j in range(8)
            ]
            for rows in work
        ]
        for k in range(8):
            for rows, cols, out in zip(work, columns, outs):
                pivot = cols[k][0][k : k + 1, :]
                inverse = 1.0 / pivot
                row = rows[g][k : k + 1, :]
                out[8 * g + k : 8 * g + k + 1, :] = row * lax.rsqrt(pivot)
                scaled = row * inverse
                for j in range(k + 1, 8):
                    factor = cols[j][0][k : k + 1, :] * inverse
                    for r in range(groups - g):
                        cols[j][r] = cols[j][r] - cols[k][r] * factor
                for r in range(g, groups):
                    column = cols[k][r - g]
                    if r == g:
                        column = jnp.where(sub > k, column, 0.0)
                    rows[r] = rows[r] - column * scaled
        if meanwhile:
            meanwhile.pop(0)()


def factor_all(mats, outs, upper):
    column = lax.broadcasted_iota(jnp.int32, (BLOCK, PAD), 1)
    row = lax.broadcasted_iota(jnp.int32, (BLOCK, PAD), 0)
    lane = lax.broadcasted_iota(jnp.int32, (BLOCK, LANES), 1)
    line = lax.broadcasted_iota(jnp.int32, (BLOCK, LANES), 0)
    steps = SKETCH // BLOCK
    meanwhile = []

    def update(mat, change, step, first, last):
        rows = slice(first * BLOCK, last * BLOCK)
        keep = lax.broadcasted_iota(jnp.int32, ((last - first) * BLOCK, PAD), 1)
        keep = (keep < step * BLOCK) | (keep >= (step + 1) * BLOCK)
        mat[rows, :] = jnp.where(keep, mat[rows, :], 0.0) - change

    for step in range(steps):
        here = slice(step * BLOCK, (step + 1) * BLOCK)
        window = slice(step // 2 * LANES, (step // 2 + 1) * LANES)
        odd = step % 2 == 1
        blocks = []
        for mat in mats:
            block = mat[here, window]
            blocks.append(pltpu.roll(block, BLOCK, 1) if odd else block)
        factor_blocks(blocks, outs, meanwhile)
        inside = (column >= step * BLOCK) & (column < (step + 1) * BLOCK)
        for n, (mat, out) in enumerate(zip(mats, outs)):
            both = out[...]
            inverse = beside(pltpu.roll(both, BLOCK, 1))
            line_up = jnp.where(inside, jnp.where(column - step * BLOCK == row, 1.0, 0.0), mat[here, :])
            panel = dot(inverse, stacked(line_up, UNDER))
            mat[here, :] = panel
            if n == 0:
                upper[here, :] = jnp.where(column >= (step + 1) * BLOCK, panel, 0.0)
                corner = jnp.where((lane < BLOCK) & (lane >= line), both, 0.0)
                corner = pltpu.roll(corner, BLOCK, 1) if odd else corner
                upper[here, window] = upper[here, window] + corner
            if step == steps - 1:
                continue
            start = (step + 1) * BLOCK // LANES * LANES
            turned = jnp.transpose(panel[:, start:])
            turned = jnp.concatenate([turned, jnp.zeros_like(turned)], axis=1)
            left, right = beside(turned), stacked(panel, UNDER)
            skip = (step + 1) * BLOCK - start
            update(mat, dot(left[skip : skip + BLOCK], right), step, step + 1, step + 2)
            if step < steps - 2:

                def rest(mat=mat, left=left, right=right, step=step, skip=skip):
                    stop = SKETCH - start_of(step)
                    update(mat, dot(left[skip + BLOCK : stop], right), step, step + 2, steps)

                def start_of(step):
                    return (step + 1) * BLOCK // LANES * LANES

                meanwhile.append(rest)


def columns_of(place, half, part, stream):
    core, mask = order(place, half, stream)
    first = (core << 4) | (stream << 3) | ((4 * part) ^ (mask & 4))
    return pl.ds(pl.multiple_of(first * LANES, WIDTH), WIDTH)


def pieces_kernel(member, id_ref, sketch_matrix_t, piece, *refs):
    before, (terms, sums, left, right, cross, mix) = refs[:-6], refs[-6:]
    place = coordinates(id_ref[0])
    _, mask = order(place, member[0], member[2])
    for slot in range(4):
        start = (slot ^ (mask & 2)) * LANES
        cross[:, pl.ds(pl.multiple_of(start, LANES), LANES)] = piece[slot]
    a, b, c = split(cross[...], 3)
    for n, (term, again) in enumerate(((a, a), (b, b), (c, a))):
        left[n * SKETCH : (n + 1) * SKETCH, :] = term
        terms[n * SKETCH : (n + 1) * SKETCH, :] = again
    right[:SKETCH, :] = a
    right[SKETCH:PAD, :] = jnp.zeros((PAD - SKETCH, WIDTH), BF16)
    right[PAD:, :] = sketch_matrix_t[:, columns_of(place, *member)]
    both = dot_nt(left[...], right[...])
    parts = [both[n * SKETCH : (n + 1) * SKETCH] for n in range(3)]
    mix[...] = jnp.zeros_like(mix)
    mix[:SKETCH, :SKETCH] = parts[1][:, :SKETCH] + parts[2][:, :SKETCH]
    mixed = (mix[...] + jnp.transpose(mix[...]))[:SKETCH]
    sums[...] = before[0][...] if before else jnp.zeros_like(sums)
    sums[0, :, :SKETCH] += parts[0][:, PAD:] + (parts[1][:, PAD:] + parts[2][:, PAD:])
    sums[1, :, :SKETCH] += parts[0][:, :SKETCH] + dot_nt(b, b)
    sums[1] += mixed


def factor_kernel(scale, id_ref, own, other, basis_map, inverse_c, gram, coupling, upper, out0, out1, wide):
    for n, ref in enumerate((gram, coupling)):
        ref[...] = jnp.zeros_like(ref)
        ref[:SKETCH, :] = own[n] + other[n]
    upper[...] = jnp.zeros_like(upper)
    factor_all((gram, coupling), (out0, out1), upper)
    row = lax.broadcasted_iota(jnp.int32, (PAD, PAD), 0)
    column = lax.broadcasted_iota(jnp.int32, (PAD, PAD), 1)
    lower = (row < SKETCH) & (column <= row)
    high, low = split(jnp.where(lower, gram[...], 0.0)[:SKETCH, :SKETCH], 2)
    for n, term in enumerate((high, high, low)):
        wide[:, n * SKETCH : (n + 1) * SKETCH] = term.astype(F32)
    basis_map[...] = wide[...].astype(BF16)
    chain = dot_three(jnp.where(lower, coupling[...], 0.0), jnp.transpose(upper[...]))
    gram[...] = dot_three(jnp.transpose(chain), chain) * scale
    inverse_c[...] = gram[:SKETCH, :SKETCH]


def final_kernel(members, id_ref, features, basis_map, inverse_c, *refs):
    terms, (result, coeffs) = refs[:-2], refs[-2:]
    place = coordinates(id_ref[0])
    for term, member in zip(terms, members):
        coeffs[:, columns_of(place, *member)] = dot(basis_map[...], term[...]).astype(BF16)
    projected = dot_nt(coeffs[...], features[...])
    result[...] = dot_three(inverse_c[...], projected)


def body(features, sketch_matrix):
    rows, width = features.shape
    rows_total = rows * lax.axis_size("rows")
    device = lax.axis_index("rows").astype(jnp.int32)[None]
    whole, piece = ((8, SKETCH, LANES), F32), ((4, SKETCH, LANES), F32)
    flops = 2 * rows * width * SKETCH

    sketch_matrix_t = sketch_matrix.T

    sketches, send0, send1 = call(
        send_kernel,
        (device, features, sketch_matrix_t),
        [((2 * SKETCH, rows), BF16), whole, whole],
        scratch=[
            pltpu.VMEM((rows, width), BF16),
            pltpu.VMEM((SKETCH, width), BF16),
            pltpu.SemaphoreType.DMA((3,)),
        ],
        flops=2 * flops,
        space=pltpu.HBM,
        limit=50,
    )
    received = across(send0), across(send1)
    low0, high0, low1, high1 = call(
        keep_kernel, (device, features, sketches), [piece] * 4, flops=flops
    )
    block = jnp.concatenate(
        [scatter_stream(0, low0, high0, received[0]), scatter_stream(1, low1, high1, received[1])]
    )
    block = jnp.sum(all_to_all(block.reshape(32, SKETCH // 8, LANES)), axis=0)
    block = all_to_all(jnp.broadcast_to(block[None], (32, *block.shape)))
    block = block.reshape(4, SKETCH, LANES)
    streams = []
    for stream in range(2):
        own = block[2 * stream : 2 * stream + 2]
        own = jnp.concatenate([own, exchange(own, stream, 1)])
        streams.append((own, exchange(own, stream, 0)))

    members = [(0, part, stream) for part in range(2) for stream in range(2)]
    terms_shape = ((3 * SKETCH, WIDTH), BF16)
    sums_shape = ((2, SKETCH, PAD), F32)
    terms, sums = [], ()
    for member in members:
        _, part, stream = member
        term, *sums = call(
            functools.partial(pieces_kernel, member),
            (device, sketch_matrix_t, streams[stream][part], *sums),
            [terms_shape, sums_shape],
            scratch=[
                pltpu.VMEM(*terms_shape),
                pltpu.VMEM((PAD + SKETCH, WIDTH), BF16),
                pltpu.VMEM((SKETCH, WIDTH), F32),
                pltpu.VMEM((PAD, PAD), F32),
            ],
        )
        terms.append(term)
    square, corner = pltpu.VMEM((PAD, PAD), F32), pltpu.VMEM((BLOCK, LANES), F32)
    basis_map, inverse_c = call(
        functools.partial(factor_kernel, math.sqrt(rows_total)),
        (device, *sums, across(*sums)),
        [((SKETCH, 3 * SKETCH), BF16), ((SKETCH, SKETCH), F32)],
        scratch=[square] * 3 + [corner] * 2 + [pltpu.VMEM((SKETCH, 3 * SKETCH), F32)],
        flops=14 * flops,
    )
    terms += [across(term) for term in terms]
    members += [(1, part, stream) for _, part, stream in members]
    (result,) = call(
        functools.partial(final_kernel, members),
        (device, features, basis_map, inverse_c, *terms),
        [((SKETCH, rows), F32)],
        scratch=[pltpu.VMEM((SKETCH, width), BF16)],
        flops=4 * flops,
    )
    return result.T


def solution(mesh):
    return jax.shard_map(
        body,
        mesh=mesh,
        in_specs=(P("rows", None), P()),
        out_specs=P("rows", None),
        check_vma=False,
    )
```

```python
import functools
import math

import jax
import jax.numpy as jnp
from jax import lax
from jax.experimental import pallas as pl
from jax.experimental.pallas import tpu as pltpu
from jax.sharding import PartitionSpec as P

SKETCH = 320
PAD = 384
BLOCK = 64
LANES = 128
WIDTH = 4 * LANES
F32 = jnp.float32
BF16 = jnp.bfloat16

FIRST_AXIS = ("y", "x")
SECOND_AXIS = ("x", "y")
Z_AXIS = ("z", "z")
STREAM_BITS = ((0, 1), (1, 0))


def coordinates(index):
    return {"c": index & 1, "x": (index >> 1) & 3, "z": (index >> 3) & 7, "y": (index >> 6) & 3}


def role_of(place):
    return place["c"] ^ ((place["x"] + place["y"] + place["z"]) & 1)


def gray(value):
    return value ^ (value >> 1)


def gray_of(place, role, axes):
    return jnp.where(role == 0, *(gray(place[axis]) for axis in axes))


def across(block):
    return lax.ppermute(block, "rows", [(i, i ^ 1) for i in range(lax.axis_size("rows"))])


def exchange(block, axes, bit):
    pairs = []
    for i in range(lax.axis_size("rows")):
        place = coordinates(i)
        role = role_of(place)
        wanted = gray(place[axes[role]]) ^ (1 << bit)
        place[axes[role]] = next(v for v in range(8) if gray(v) == wanted)
        place["c"] ^= role ^ role_of(place)
        there = ((place["y"] * 8 + place["z"]) * 4 + place["x"]) * 2 + place["c"]
        pairs.append((i, there))
    return lax.ppermute(block, "rows", pairs)


def halve(block, place, axes, bit):
    low, high = jnp.split(block, 2)
    upper = (gray_of(place, role_of(place), axes) >> bit) & 1
    sent = exchange(jnp.where(upper == 0, high, low), axes, bit)
    return jnp.where(upper == 0, low, high) + sent


def double(block, place, axes, bit):
    upper = (gray_of(place, role_of(place), axes) >> bit) & 1
    other = exchange(block, axes, bit)
    return jnp.concatenate([jnp.where(upper == 0, block, other), jnp.where(upper == 0, other, block)])


def inner_sum(block, place):
    block = halve(block, place, SECOND_AXIS, 1)
    block = halve(block, place, SECOND_AXIS, 0)[0]
    block = halve(block, place, Z_AXIS, 0)
    for bit in (1, 2):
        block = block + exchange(block, Z_AXIS, bit)
    block = double(block, place, Z_AXIS, 0)[None]
    block = double(block, place, SECOND_AXIS, 0)
    return double(block, place, SECOND_AXIS, 1)


def order(place, half, stream):
    role = role_of(place) ^ half
    code = gray_of(place, role, FIRST_AXIS)
    first, second = STREAM_BITS[stream]
    return role, (((code >> first) & 1) << 2) | (((code >> second) & 1) << 1)


def cross_blocks(id_ref, features, sketches, outs):
    place = coordinates(id_ref[0])
    for (half, stream, start), out in outs:
        role, mask = order(place, half, stream)
        for pair in range(out.shape[0] // 2):
            there = (role << 4) | (stream << 3) | ((start + 2 * pair) ^ mask)
            columns = features[:, pl.ds(pl.multiple_of(there * LANES, 256), 256)]
            both = jnp.dot(sketches[...], columns, preferred_element_type=F32)
            cross = both[:SKETCH] + both[SKETCH:]
            out[2 * pair] = cross[:, :LANES]
            out[2 * pair + 1] = cross[:, LANES:]


def send_kernel(id_ref, features_hbm, matrix_hbm, sketches, send0, send1, features, matrix, sems):
    chunks = sems.shape[1]
    width = features.shape[1] // chunks
    copies = []
    for n in range(chunks):
        columns = slice(n * width, (n + 1) * width)
        pair = [
            pltpu.make_async_copy(source.at[:, columns], target.at[:, columns], sems.at[m, n])
            for m, (source, target) in enumerate(((matrix_hbm, matrix), (features_hbm, features)))
        ]
        for copy in pair:
            copy.start()
        copies.append((columns, pair))
    sketch_t = jnp.zeros((SKETCH, features.shape[0]), F32)
    for columns, pair in copies:
        for copy in pair:
            copy.wait()
        sketch_t += dot_nt(matrix[:, columns], features[:, columns])
    high, low = split(sketch_t, 2)
    sketches[:SKETCH, :] = high
    sketches[SKETCH:, :] = low
    cross_blocks(id_ref, features, sketches, (((1, 0, 0), send0), ((1, 1, 0), send1)))


def keep_kernel(id_ref, features, sketches, low0, high0, low1, high1):
    wanted = ((0, 0, 0), (0, 0, 4), (0, 1, 0), (0, 1, 4))
    cross_blocks(id_ref, features, sketches, tuple(zip(wanted, (low0, high0, low1, high1))))


def call(kernel, operands, outs, scratch=(), flops=0, limit=24, space=pltpu.VMEM):
    vmem = pl.BlockSpec(memory_space=pltpu.VMEM)
    return pl.pallas_call(
        kernel,
        out_shape=[jax.ShapeDtypeStruct(shape, dtype) for shape, dtype in outs],
        in_specs=[pl.BlockSpec(memory_space=pltpu.SMEM)]
        + [pl.BlockSpec(memory_space=space)] * (len(operands) - 1),
        out_specs=[vmem] * len(outs),
        scratch_shapes=scratch,
        compiler_params=pltpu.CompilerParams(vmem_limit_bytes=limit * 1024 * 1024),
        cost_estimate=pl.CostEstimate(flops=flops, bytes_accessed=4 * 1024 * 1024, transcendentals=0),
    )(*operands)


def scatter_stream(stream, low, high, received):
    first, second = STREAM_BITS[stream]
    back = exchange(high + received[4:], FIRST_AXIS, first)
    block = low + received[:4]
    back_next = exchange(block[2:] + back[2:], FIRST_AXIS, second)
    return block[:2] + back[:2] + back_next


def split(value, terms):
    parts = []
    for _ in range(terms):
        part = value.astype(BF16)
        parts.append(part)
        value = value - part.astype(F32)
    return parts


def dot_nt(a, b, precision=None):
    return lax.dot_general(
        a, b, (((1,), (1,)), ((), ())), precision=precision, preferred_element_type=F32
    )


def dot(a, b, precision=None):
    return jnp.dot(a, b, precision=precision, preferred_element_type=F32)


def dot_three(a, b):
    a0, a1 = split(a, 2)
    b0, b1 = split(b, 2)
    return dot(a0, b0) + (dot(a0, b1) + dot(a1, b0))


def stacked(rows, terms):
    parts = split(rows, 3)
    return jnp.concatenate([parts[n] for n in terms], axis=0)


def beside(value):
    lane = lax.broadcasted_iota(jnp.int32, value.shape, 1)
    parts = [part.astype(F32) for part in split(value, 3)]
    turned = [pltpu.roll(part, BLOCK, 1) for part in parts[:2]]
    pairs = ((0, 0), (1, 0), (2, 1))
    return jnp.concatenate(
        [jnp.where(lane < BLOCK, parts[m], turned[n]).astype(BF16) for m, n in pairs], axis=1
    )


UNDER = (0, 1, 0, 2, 0, 1)


def factor_blocks(blocks, outs, meanwhile):
    groups = BLOCK // 8
    lane = lax.broadcasted_iota(jnp.int32, (8, LANES), 1)
    sub = lax.broadcasted_iota(jnp.int32, (8, LANES), 0)
    work = []
    for block in blocks:
        rows = []
        for g in range(groups):
            unit = jnp.where(lane - BLOCK == sub + 8 * g, 1.0, 0.0).astype(F32)
            rows.append(jnp.where(lane < BLOCK, block[8 * g : 8 * g + 8], unit))
        work.append(rows)
    for g in range(groups):
        columns = [
            [
                [
                    jnp.broadcast_to(rows[r][:, 8 * g + j : 8 * g + j + 1], (8, LANES))
                    for r in range(g, groups)
                ]
                for j in range(8)
            ]
            for rows in work
        ]
        for k in range(8):
            for rows, cols, out in zip(work, columns, outs):
                pivot = cols[k][0][k : k + 1, :]
                inverse = 1.0 / pivot
                row = rows[g][k : k + 1, :]
                out[8 * g + k : 8 * g + k + 1, :] = row * lax.rsqrt(pivot)
                scaled = row * inverse
                for j in range(k + 1, 8):
                    factor = cols[j][0][k : k + 1, :] * inverse
                    for r in range(groups - g):
                        cols[j][r] = cols[j][r] - cols[k][r] * factor
                for r in range(g, groups):
                    column = cols[k][r - g]
                    if r == g:
                        column = jnp.where(sub > k, column, 0.0)
                    rows[r] = rows[r] - column * scaled
        if meanwhile:
            meanwhile.pop(0)()


def factor_all(mats, outs, upper):
    column = lax.broadcasted_iota(jnp.int32, (BLOCK, PAD), 1)
    row = lax.broadcasted_iota(jnp.int32, (BLOCK, PAD), 0)
    lane = lax.broadcasted_iota(jnp.int32, (BLOCK, LANES), 1)
    line = lax.broadcasted_iota(jnp.int32, (BLOCK, LANES), 0)
    steps = SKETCH // BLOCK
    meanwhile = []

    def update(mat, change, step, first, last):
        rows = slice(first * BLOCK, last * BLOCK)
        keep = lax.broadcasted_iota(jnp.int32, ((last - first) * BLOCK, PAD), 1)
        keep = (keep < step * BLOCK) | (keep >= (step + 1) * BLOCK)
        mat[rows, :] = jnp.where(keep, mat[rows, :], 0.0) - change

    for step in range(steps):
        here = slice(step * BLOCK, (step + 1) * BLOCK)
        window = slice(step // 2 * LANES, (step // 2 + 1) * LANES)
        odd = step % 2 == 1
        blocks = []
        for mat in mats:
            block = mat[here, window]
            blocks.append(pltpu.roll(block, BLOCK, 1) if odd else block)
        factor_blocks(blocks, outs, meanwhile)
        inside = (column >= step * BLOCK) & (column < (step + 1) * BLOCK)
        for n, (mat, out) in enumerate(zip(mats, outs)):
            both = out[...]
            inverse = beside(pltpu.roll(both, BLOCK, 1))
            line_up = jnp.where(inside, jnp.where(column - step * BLOCK == row, 1.0, 0.0), mat[here, :])
            panel = dot(inverse, stacked(line_up, UNDER))
            mat[here, :] = panel
            if n == 0:
                upper[here, :] = jnp.where(column >= (step + 1) * BLOCK, panel, 0.0)
                corner = jnp.where((lane < BLOCK) & (lane >= line), both, 0.0)
                corner = pltpu.roll(corner, BLOCK, 1) if odd else corner
                upper[here, window] = upper[here, window] + corner
            if step == steps - 1:
                continue
            start = (step + 1) * BLOCK // LANES * LANES
            turned = jnp.transpose(panel[:, start:])
            turned = jnp.concatenate([turned, jnp.zeros_like(turned)], axis=1)
            left, right = beside(turned), stacked(panel, UNDER)
            skip = (step + 1) * BLOCK - start
            update(mat, dot(left[skip : skip + BLOCK], right), step, step + 1, step + 2)
            if step < steps - 2:

                def rest(mat=mat, left=left, right=right, step=step, skip=skip):
                    stop = SKETCH - start_of(step)
                    update(mat, dot(left[skip + BLOCK : stop], right), step, step + 2, steps)

                def start_of(step):
                    return (step + 1) * BLOCK // LANES * LANES

                meanwhile.append(rest)


def columns_of(place, half, part, stream):
    role, mask = order(place, half, stream)
    first = (role << 4) | (stream << 3) | ((4 * part) ^ (mask & 4))
    return pl.ds(pl.multiple_of(first * LANES, WIDTH), WIDTH)


def pieces_kernel(member, id_ref, sketch_matrix_t, piece, *refs):
    before, (terms, sums, left, right, cross, mix) = refs[:-6], refs[-6:]
    place = coordinates(id_ref[0])
    _, mask = order(place, member[0], member[2])
    for slot in range(4):
        start = (slot ^ (mask & 2)) * LANES
        cross[:, pl.ds(pl.multiple_of(start, LANES), LANES)] = piece[slot]
    a, b, c = split(cross[...], 3)
    for n, (term, again) in enumerate(((a, a), (b, b), (c, a))):
        left[n * SKETCH : (n + 1) * SKETCH, :] = term
        terms[n * SKETCH : (n + 1) * SKETCH, :] = again
    right[:SKETCH, :] = a
    right[SKETCH:PAD, :] = jnp.zeros((PAD - SKETCH, WIDTH), BF16)
    right[PAD:, :] = sketch_matrix_t[:, columns_of(place, *member)]
    both = dot_nt(left[...], right[...])
    parts = [both[n * SKETCH : (n + 1) * SKETCH] for n in range(3)]
    mix[...] = jnp.zeros_like(mix)
    mix[:SKETCH, :SKETCH] = parts[1][:, :SKETCH] + parts[2][:, :SKETCH]
    mixed = (mix[...] + jnp.transpose(mix[...]))[:SKETCH]
    sums[...] = before[0][...] if before else jnp.zeros_like(sums)
    sums[0, :, :SKETCH] += parts[0][:, PAD:] + (parts[1][:, PAD:] + parts[2][:, PAD:])
    sums[1, :, :SKETCH] += parts[0][:, :SKETCH] + dot_nt(b, b)
    sums[1] += mixed


def factor_kernel(scale, id_ref, own, other, basis_map, inverse_c, gram, coupling, upper, out0, out1, wide):
    for n, ref in enumerate((gram, coupling)):
        ref[...] = jnp.zeros_like(ref)
        ref[:SKETCH, :] = own[n] + other[n]
    upper[...] = jnp.zeros_like(upper)
    factor_all((gram, coupling), (out0, out1), upper)
    row = lax.broadcasted_iota(jnp.int32, (PAD, PAD), 0)
    column = lax.broadcasted_iota(jnp.int32, (PAD, PAD), 1)
    lower = (row < SKETCH) & (column <= row)
    high, low = split(jnp.where(lower, gram[...], 0.0)[:SKETCH, :SKETCH], 2)
    for n, term in enumerate((high, high, low)):
        wide[:, n * SKETCH : (n + 1) * SKETCH] = term.astype(F32)
    basis_map[...] = wide[...].astype(BF16)
    chain = dot_three(jnp.where(lower, coupling[...], 0.0), jnp.transpose(upper[...]))
    gram[...] = dot_three(jnp.transpose(chain), chain) * scale
    inverse_c[...] = gram[:SKETCH, :SKETCH]


def final_kernel(members, id_ref, features, basis_map, inverse_c, *refs):
    terms, (result, coeffs) = refs[:-2], refs[-2:]
    place = coordinates(id_ref[0])
    for term, member in zip(terms, members):
        coeffs[:, columns_of(place, *member)] = dot(basis_map[...], term[...]).astype(BF16)
    projected = dot_nt(coeffs[...], features[...])
    result[...] = dot_three(inverse_c[...], projected)


def body(features, sketch_matrix):
    rows, width = features.shape
    rows_total = rows * lax.axis_size("rows")
    device = lax.axis_index("rows").astype(jnp.int32)[None]
    whole, piece = ((8, SKETCH, LANES), F32), ((4, SKETCH, LANES), F32)
    flops = 2 * rows * width * SKETCH

    sketch_matrix_t = sketch_matrix.T

    sketches, send0, send1 = call(
        send_kernel,
        (device, features, sketch_matrix_t),
        [((2 * SKETCH, rows), BF16), whole, whole],
        scratch=[
            pltpu.VMEM((rows, width), BF16),
            pltpu.VMEM((SKETCH, width), BF16),
            pltpu.SemaphoreType.DMA((2, 4)),
        ],
        flops=2 * flops,
        space=pltpu.HBM,
        limit=50,
    )
    received = across(send0), across(send1)
    low0, high0, low1, high1 = call(
        keep_kernel, (device, features, sketches), [piece] * 4, flops=flops
    )
    block = jnp.concatenate(
        [scatter_stream(0, low0, high0, received[0]), scatter_stream(1, low1, high1, received[1])]
    )
    block = inner_sum(block, coordinates(device[0]))
    streams = []
    for stream, (first, second) in enumerate(STREAM_BITS):
        own = block[2 * stream : 2 * stream + 2]
        own = jnp.concatenate([own, exchange(own, FIRST_AXIS, second)])
        streams.append((own, exchange(own, FIRST_AXIS, first)))

    members = [(0, part, stream) for part in range(2) for stream in range(2)]
    terms_shape = ((3 * SKETCH, WIDTH), BF16)
    sums_shape = ((2, SKETCH, PAD), F32)
    terms, sums = [], ()
    for member in members:
        _, part, stream = member
        term, *sums = call(
            functools.partial(pieces_kernel, member),
            (device, sketch_matrix_t, streams[stream][part], *sums),
            [terms_shape, sums_shape],
            scratch=[
                pltpu.VMEM(*terms_shape),
                pltpu.VMEM((PAD + SKETCH, WIDTH), BF16),
                pltpu.VMEM((SKETCH, WIDTH), F32),
                pltpu.VMEM((PAD, PAD), F32),
            ],
        )
        terms.append(term)
    square, corner = pltpu.VMEM((PAD, PAD), F32), pltpu.VMEM((BLOCK, LANES), F32)
    basis_map, inverse_c = call(
        functools.partial(factor_kernel, math.sqrt(rows_total)),
        (device, *sums, across(*sums)),
        [((SKETCH, 3 * SKETCH), BF16), ((SKETCH, SKETCH), F32)],
        scratch=[square] * 3 + [corner] * 2 + [pltpu.VMEM((SKETCH, 3 * SKETCH), F32)],
        flops=14 * flops,
    )
    terms += [across(term) for term in terms]
    members += [(1, part, stream) for _, part, stream in members]
    (result,) = call(
        functools.partial(final_kernel, members),
        (device, features, basis_map, inverse_c, *terms),
        [((SKETCH, rows), F32)],
        scratch=[pltpu.VMEM((SKETCH, width), BF16)],
        flops=4 * flops,
    )
    return result.T


def solution(mesh):
    return jax.shard_map(
        body,
        mesh=mesh,
        in_specs=(P("rows", None), P()),
        out_specs=P("rows", None),
        check_vma=False,
    )
```

```python
import functools
import math

import jax
import jax.numpy as jnp
from jax import lax
from jax.experimental import pallas as pl
from jax.experimental.pallas import tpu as pltpu
from jax.sharding import PartitionSpec as P

SKETCH = 320
PAD = 384
BLOCK = 64
LANES = 128
WIDTH = 4 * LANES
F32 = jnp.float32
BF16 = jnp.bfloat16

FIRST_AXIS = ("y", "x")
SECOND_AXIS = ("x", "y")
Z_AXIS = ("z", "z")
STREAM_BITS = ((0, 1), (1, 0))


def coordinates(index):
    return {"c": index & 1, "x": (index >> 1) & 3, "z": (index >> 3) & 7, "y": (index >> 6) & 3}


def role_of(place):
    return place["c"] ^ ((place["x"] + place["y"] + place["z"]) & 1)


def gray(value):
    return value ^ (value >> 1)


def gray_of(place, role, axes):
    return jnp.where(role == 0, *(gray(place[axis]) for axis in axes))


def across(block):
    return lax.ppermute(block, "rows", [(i, i ^ 1) for i in range(lax.axis_size("rows"))])


def exchange(block, axes, bit):
    pairs = []
    for i in range(lax.axis_size("rows")):
        place = coordinates(i)
        role = role_of(place)
        wanted = gray(place[axes[role]]) ^ (1 << bit)
        place[axes[role]] = next(v for v in range(8) if gray(v) == wanted)
        place["c"] ^= role ^ role_of(place)
        there = ((place["y"] * 8 + place["z"]) * 4 + place["x"]) * 2 + place["c"]
        pairs.append((i, there))
    return lax.ppermute(block, "rows", pairs)


def shifted(block, axes, shift):
    pairs = []
    for i in range(lax.axis_size("rows")):
        place = coordinates(i)
        role = role_of(place)
        place[axes[role]] = (place[axes[role]] + shift) % 4
        place["c"] ^= role ^ role_of(place)
        there = ((place["y"] * 8 + place["z"]) * 4 + place["x"]) * 2 + place["c"]
        pairs.append((i, there))
    return lax.ppermute(block, "rows", pairs)


def ring_scatter(blocks, place):
    own = jnp.where(role_of(place) == 0, *(place[axis] for axis in SECOND_AXIS))
    pick = lambda n: lax.dynamic_index_in_dim(blocks, (own + n) & 3, 0, keepdims=False)
    received = [shifted(pick(n), SECOND_AXIS, n) for n in (1, 3, 2)]
    return (pick(0) + received[0]) + (received[1] + received[2])


def ring_gather(block, place):
    own = jnp.where(role_of(place) == 0, *(place[axis] for axis in SECOND_AXIS))
    received = [(n, shifted(block, SECOND_AXIS, -n)) for n in (1, 3, 2)]
    blocks = jnp.zeros((4, *block.shape), F32)
    for n, part in [(0, block)] + received:
        blocks = lax.dynamic_update_index_in_dim(blocks, part, (own + n) & 3, 0)
    return blocks


def halve(block, place, axes, bit):
    low, high = jnp.split(block, 2)
    upper = (gray_of(place, role_of(place), axes) >> bit) & 1
    sent = exchange(jnp.where(upper == 0, high, low), axes, bit)
    return jnp.where(upper == 0, low, high) + sent


def double(block, place, axes, bit):
    upper = (gray_of(place, role_of(place), axes) >> bit) & 1
    other = exchange(block, axes, bit)
    return jnp.concatenate([jnp.where(upper == 0, block, other), jnp.where(upper == 0, other, block)])


def inner_sum(block, place):
    block = ring_scatter(block, place)
    block = halve(block, place, Z_AXIS, 0)
    for bit in (1, 2):
        block = block + exchange(block, Z_AXIS, bit)
    return ring_gather(double(block, place, Z_AXIS, 0), place)


def order(place, half, stream):
    role = role_of(place) ^ half
    code = gray_of(place, role, FIRST_AXIS)
    first, second = STREAM_BITS[stream]
    return role, (((code >> first) & 1) << 2) | (((code >> second) & 1) << 1)


def cross_blocks(id_ref, features, sketches, outs):
    place = coordinates(id_ref[0])
    for (half, stream, start), out in outs:
        role, mask = order(place, half, stream)
        for pair in range(out.shape[0] // 2):
            there = (role << 4) | (stream << 3) | ((start + 2 * pair) ^ mask)
            columns = features[:, pl.ds(pl.multiple_of(there * LANES, 256), 256)]
            both = jnp.dot(sketches[...], columns, preferred_element_type=F32)
            cross = both[:SKETCH] + both[SKETCH:]
            out[2 * pair] = cross[:, :LANES]
            out[2 * pair + 1] = cross[:, LANES:]


def send_kernel(id_ref, features_hbm, matrix_hbm, sketches, send0, send1, features, matrix, sems):
    chunks = sems.shape[1]
    width = features.shape[1] // chunks
    copies = []
    for n in range(chunks):
        columns = slice(n * width, (n + 1) * width)
        pair = [
            pltpu.make_async_copy(source.at[:, columns], target.at[:, columns], sems.at[m, n])
            for m, (source, target) in enumerate(((matrix_hbm, matrix), (features_hbm, features)))
        ]
        for copy in pair:
            copy.start()
        copies.append((columns, pair))
    sketch_t = jnp.zeros((SKETCH, features.shape[0]), F32)
    for columns, pair in copies:
        for copy in pair:
            copy.wait()
        sketch_t += dot_nt(matrix[:, columns], features[:, columns])
    high, low = split(sketch_t, 2)
    sketches[:SKETCH, :] = high
    sketches[SKETCH:, :] = low
    cross_blocks(id_ref, features, sketches, (((1, 0, 0), send0), ((1, 1, 0), send1)))


def keep_kernel(id_ref, features, sketches, low0, high0, low1, high1):
    wanted = ((0, 0, 0), (0, 0, 4), (0, 1, 0), (0, 1, 4))
    cross_blocks(id_ref, features, sketches, tuple(zip(wanted, (low0, high0, low1, high1))))


def call(kernel, operands, outs, scratch=(), flops=0, limit=24, space=pltpu.VMEM):
    vmem = pl.BlockSpec(memory_space=pltpu.VMEM)
    return pl.pallas_call(
        kernel,
        out_shape=[jax.ShapeDtypeStruct(shape, dtype) for shape, dtype in outs],
        in_specs=[pl.BlockSpec(memory_space=pltpu.SMEM)]
        + [pl.BlockSpec(memory_space=space)] * (len(operands) - 1),
        out_specs=[vmem] * len(outs),
        scratch_shapes=scratch,
        compiler_params=pltpu.CompilerParams(vmem_limit_bytes=limit * 1024 * 1024),
        cost_estimate=pl.CostEstimate(flops=flops, bytes_accessed=4 * 1024 * 1024, transcendentals=0),
    )(*operands)


def scatter_stream(stream, low, high, received):
    first, second = STREAM_BITS[stream]
    back = exchange(high + received[4:], FIRST_AXIS, first)
    block = low + received[:4]
    back_next = exchange(block[2:] + back[2:], FIRST_AXIS, second)
    return block[:2] + back[:2] + back_next


def split(value, terms):
    parts = []
    for _ in range(terms):
        part = value.astype(BF16)
        parts.append(part)
        value = value - part.astype(F32)
    return parts


def dot_nt(a, b, precision=None):
    return lax.dot_general(
        a, b, (((1,), (1,)), ((), ())), precision=precision, preferred_element_type=F32
    )


def dot(a, b, precision=None):
    return jnp.dot(a, b, precision=precision, preferred_element_type=F32)


def dot_three(a, b):
    a0, a1 = split(a, 2)
    b0, b1 = split(b, 2)
    return dot(a0, b0) + (dot(a0, b1) + dot(a1, b0))


def stacked(rows, terms):
    parts = split(rows, 3)
    return jnp.concatenate([parts[n] for n in terms], axis=0)


def beside(value):
    lane = lax.broadcasted_iota(jnp.int32, value.shape, 1)
    parts = [part.astype(F32) for part in split(value, 3)]
    turned = [pltpu.roll(part, BLOCK, 1) for part in parts[:2]]
    pairs = ((0, 0), (1, 0), (2, 1))
    return jnp.concatenate(
        [jnp.where(lane < BLOCK, parts[m], turned[n]).astype(BF16) for m, n in pairs], axis=1
    )


UNDER = (0, 1, 0, 2, 0, 1)


def factor_blocks(blocks, outs, meanwhile):
    groups = BLOCK // 8
    lane = lax.broadcasted_iota(jnp.int32, (8, LANES), 1)
    sub = lax.broadcasted_iota(jnp.int32, (8, LANES), 0)
    work = []
    for block in blocks:
        rows = []
        for g in range(groups):
            unit = jnp.where(lane - BLOCK == sub + 8 * g, 1.0, 0.0).astype(F32)
            rows.append(jnp.where(lane < BLOCK, block[8 * g : 8 * g + 8], unit))
        work.append(rows)
    for g in range(groups):
        columns = [
            [
                [
                    jnp.broadcast_to(rows[r][:, 8 * g + j : 8 * g + j + 1], (8, LANES))
                    for r in range(g, groups)
                ]
                for j in range(8)
            ]
            for rows in work
        ]
        for k in range(8):
            for rows, cols, out in zip(work, columns, outs):
                pivot = cols[k][0][k : k + 1, :]
                inverse = 1.0 / pivot
                row = rows[g][k : k + 1, :]
                out[8 * g + k : 8 * g + k + 1, :] = row * lax.rsqrt(pivot)
                scaled = row * inverse
                for j in range(k + 1, 8):
                    factor = cols[j][0][k : k + 1, :] * inverse
                    for r in range(groups - g):
                        cols[j][r] = cols[j][r] - cols[k][r] * factor
                for r in range(g, groups):
                    column = cols[k][r - g]
                    if r == g:
                        column = jnp.where(sub > k, column, 0.0)
                    rows[r] = rows[r] - column * scaled
        if meanwhile:
            meanwhile.pop(0)()


def factor_all(mats, outs, upper):
    column = lax.broadcasted_iota(jnp.int32, (BLOCK, PAD), 1)
    row = lax.broadcasted_iota(jnp.int32, (BLOCK, PAD), 0)
    lane = lax.broadcasted_iota(jnp.int32, (BLOCK, LANES), 1)
    line = lax.broadcasted_iota(jnp.int32, (BLOCK, LANES), 0)
    steps = SKETCH // BLOCK
    meanwhile = []

    def update(mat, change, step, first, last):
        rows = slice(first * BLOCK, last * BLOCK)
        keep = lax.broadcasted_iota(jnp.int32, ((last - first) * BLOCK, PAD), 1)
        keep = (keep < step * BLOCK) | (keep >= (step + 1) * BLOCK)
        mat[rows, :] = jnp.where(keep, mat[rows, :], 0.0) - change

    for step in range(steps):
        here = slice(step * BLOCK, (step + 1) * BLOCK)
        window = slice(step // 2 * LANES, (step // 2 + 1) * LANES)
        odd = step % 2 == 1
        blocks = []
        for mat in mats:
            block = mat[here, window]
            blocks.append(pltpu.roll(block, BLOCK, 1) if odd else block)
        factor_blocks(blocks, outs, meanwhile)
        inside = (column >= step * BLOCK) & (column < (step + 1) * BLOCK)
        for n, (mat, out) in enumerate(zip(mats, outs)):
            both = out[...]
            inverse = beside(pltpu.roll(both, BLOCK, 1))
            line_up = jnp.where(inside, jnp.where(column - step * BLOCK == row, 1.0, 0.0), mat[here, :])
            panel = dot(inverse, stacked(line_up, UNDER))
            mat[here, :] = panel
            if n == 0:
                upper[here, :] = jnp.where(column >= (step + 1) * BLOCK, panel, 0.0)
                corner = jnp.where((lane < BLOCK) & (lane >= line), both, 0.0)
                corner = pltpu.roll(corner, BLOCK, 1) if odd else corner
                upper[here, window] = upper[here, window] + corner
            if step == steps - 1:
                continue
            start = (step + 1) * BLOCK // LANES * LANES
            turned = jnp.transpose(panel[:, start:])
            turned = jnp.concatenate([turned, jnp.zeros_like(turned)], axis=1)
            left, right = beside(turned), stacked(panel, UNDER)
            skip = (step + 1) * BLOCK - start
            update(mat, dot(left[skip : skip + BLOCK], right), step, step + 1, step + 2)
            if step < steps - 2:

                def rest(mat=mat, left=left, right=right, step=step, skip=skip):
                    stop = SKETCH - start_of(step)
                    update(mat, dot(left[skip + BLOCK : stop], right), step, step + 2, steps)

                def start_of(step):
                    return (step + 1) * BLOCK // LANES * LANES

                meanwhile.append(rest)


def columns_of(place, half, part, stream):
    role, mask = order(place, half, stream)
    first = (role << 4) | (stream << 3) | ((4 * part) ^ (mask & 4))
    return pl.ds(pl.multiple_of(first * LANES, WIDTH), WIDTH)


def pieces_kernel(member, id_ref, sketch_matrix_t, piece, *refs):
    before, (terms, sums, left, right, cross, mix) = refs[:-6], refs[-6:]
    place = coordinates(id_ref[0])
    _, mask = order(place, member[0], member[2])
    for slot in range(4):
        start = (slot ^ (mask & 2)) * LANES
        cross[:, pl.ds(pl.multiple_of(start, LANES), LANES)] = piece[slot]
    a, b, c = split(cross[...], 3)
    for n, (term, again) in enumerate(((a, a), (b, b), (c, a))):
        left[n * SKETCH : (n + 1) * SKETCH, :] = term
        terms[n * SKETCH : (n + 1) * SKETCH, :] = again
    right[:SKETCH, :] = a
    right[SKETCH:PAD, :] = jnp.zeros((PAD - SKETCH, WIDTH), BF16)
    right[PAD:, :] = sketch_matrix_t[:, columns_of(place, *member)]
    both = dot_nt(left[...], right[...])
    parts = [both[n * SKETCH : (n + 1) * SKETCH] for n in range(3)]
    mix[...] = jnp.zeros_like(mix)
    mix[:SKETCH, :SKETCH] = parts[1][:, :SKETCH] + parts[2][:, :SKETCH]
    mixed = (mix[...] + jnp.transpose(mix[...]))[:SKETCH]
    sums[...] = before[0][...] if before else jnp.zeros_like(sums)
    sums[0, :, :SKETCH] += parts[0][:, PAD:] + (parts[1][:, PAD:] + parts[2][:, PAD:])
    sums[1, :, :SKETCH] += parts[0][:, :SKETCH] + dot_nt(b, b)
    sums[1] += mixed


def factor_kernel(scale, id_ref, own, other, basis_map, inverse_c, gram, coupling, upper, out0, out1, wide):
    for n, ref in enumerate((gram, coupling)):
        ref[...] = jnp.zeros_like(ref)
        ref[:SKETCH, :] = own[n] + other[n]
    upper[...] = jnp.zeros_like(upper)
    factor_all((gram, coupling), (out0, out1), upper)
    row = lax.broadcasted_iota(jnp.int32, (PAD, PAD), 0)
    column = lax.broadcasted_iota(jnp.int32, (PAD, PAD), 1)
    lower = (row < SKETCH) & (column <= row)
    high, low = split(jnp.where(lower, gram[...], 0.0)[:SKETCH, :SKETCH], 2)
    for n, term in enumerate((high, high, low)):
        wide[:, n * SKETCH : (n + 1) * SKETCH] = term.astype(F32)
    basis_map[...] = wide[...].astype(BF16)
    chain = dot_three(jnp.where(lower, coupling[...], 0.0), jnp.transpose(upper[...]))
    gram[...] = dot_three(jnp.transpose(chain), chain) * scale
    inverse_c[...] = gram[:SKETCH, :SKETCH]


def final_kernel(members, id_ref, features, basis_map, inverse_c, *refs):
    terms, (result, coeffs) = refs[:-2], refs[-2:]
    place = coordinates(id_ref[0])
    for term, member in zip(terms, members):
        coeffs[:, columns_of(place, *member)] = dot(basis_map[...], term[...]).astype(BF16)
    projected = dot_nt(coeffs[...], features[...])
    result[...] = dot_three(inverse_c[...], projected)


def body(features, sketch_matrix):
    rows, width = features.shape
    rows_total = rows * lax.axis_size("rows")
    device = lax.axis_index("rows").astype(jnp.int32)[None]
    whole, piece = ((8, SKETCH, LANES), F32), ((4, SKETCH, LANES), F32)
    flops = 2 * rows * width * SKETCH

    sketch_matrix_t = sketch_matrix.T

    sketches, send0, send1 = call(
        send_kernel,
        (device, features, sketch_matrix_t),
        [((2 * SKETCH, rows), BF16), whole, whole],
        scratch=[
            pltpu.VMEM((rows, width), BF16),
            pltpu.VMEM((SKETCH, width), BF16),
            pltpu.SemaphoreType.DMA((2, 4)),
        ],
        flops=2 * flops,
        space=pltpu.HBM,
        limit=50,
    )
    received = across(send0), across(send1)
    low0, high0, low1, high1 = call(
        keep_kernel, (device, features, sketches), [piece] * 4, flops=flops
    )
    block = jnp.concatenate(
        [scatter_stream(0, low0, high0, received[0]), scatter_stream(1, low1, high1, received[1])]
    )
    block = inner_sum(block, coordinates(device[0]))
    streams = []
    for stream, (first, second) in enumerate(STREAM_BITS):
        own = block[2 * stream : 2 * stream + 2]
        own = jnp.concatenate([own, exchange(own, FIRST_AXIS, second)])
        streams.append((own, exchange(own, FIRST_AXIS, first)))

    members = [(0, part, stream) for part in range(2) for stream in range(2)]
    terms_shape = ((3 * SKETCH, WIDTH), BF16)
    sums_shape = ((2, SKETCH, PAD), F32)
    terms, sums = [], ()
    for member in members:
        _, part, stream = member
        term, *sums = call(
            functools.partial(pieces_kernel, member),
            (device, sketch_matrix_t, streams[stream][part], *sums),
            [terms_shape, sums_shape],
            scratch=[
                pltpu.VMEM(*terms_shape),
                pltpu.VMEM((PAD + SKETCH, WIDTH), BF16),
                pltpu.VMEM((SKETCH, WIDTH), F32),
                pltpu.VMEM((PAD, PAD), F32),
            ],
        )
        terms.append(term)
    square, corner = pltpu.VMEM((PAD, PAD), F32), pltpu.VMEM((BLOCK, LANES), F32)
    basis_map, inverse_c = call(
        functools.partial(factor_kernel, math.sqrt(rows_total)),
        (device, *sums, across(*sums)),
        [((SKETCH, 3 * SKETCH), BF16), ((SKETCH, SKETCH), F32)],
        scratch=[square] * 3 + [corner] * 2 + [pltpu.VMEM((SKETCH, 3 * SKETCH), F32)],
        flops=14 * flops,
    )
    terms += [across(term) for term in terms]
    members += [(1, part, stream) for _, part, stream in members]
    (result,) = call(
        functools.partial(final_kernel, members),
        (device, features, basis_map, inverse_c, *terms),
        [((SKETCH, rows), F32)],
        scratch=[pltpu.VMEM((SKETCH, width), BF16)],
        flops=4 * flops,
    )
    return result.T


def solution(mesh):
    return jax.shard_map(
        body,
        mesh=mesh,
        in_specs=(P("rows", None), P()),
        out_specs=P("rows", None),
        check_vma=False,
    )
```

```python
import functools
import math

import jax
import jax.numpy as jnp
from jax import lax
from jax.experimental import pallas as pl
from jax.experimental.pallas import tpu as pltpu
from jax.sharding import PartitionSpec as P

SKETCH = 320
PAD = 384
BLOCK = 64
LANES = 128
WIDTH = 4 * LANES
F32 = jnp.float32
BF16 = jnp.bfloat16

FIRST_AXIS = ("y", "x")
SECOND_AXIS = ("x", "y")
Z_AXIS = ("z", "z")
STREAM_BITS = ((0, 1), (1, 0))


def coordinates(index):
    return {"c": index & 1, "x": (index >> 1) & 3, "z": (index >> 3) & 7, "y": (index >> 6) & 3}


def role_of(place):
    return place["c"] ^ ((place["x"] + place["y"] + place["z"]) & 1)


def gray(value):
    return value ^ (value >> 1)


def gray_of(place, role, axes):
    return jnp.where(role == 0, *(gray(place[axis]) for axis in axes))


def across(block):
    return lax.ppermute(block, "rows", [(i, i ^ 1) for i in range(lax.axis_size("rows"))])


def exchange(block, axes, bit):
    pairs = []
    for i in range(lax.axis_size("rows")):
        place = coordinates(i)
        role = role_of(place)
        wanted = gray(place[axes[role]]) ^ (1 << bit)
        place[axes[role]] = next(v for v in range(8) if gray(v) == wanted)
        place["c"] ^= role ^ role_of(place)
        there = ((place["y"] * 8 + place["z"]) * 4 + place["x"]) * 2 + place["c"]
        pairs.append((i, there))
    return lax.ppermute(block, "rows", pairs)


def shifted(block, axes, shift):
    pairs = []
    for i in range(lax.axis_size("rows")):
        place = coordinates(i)
        role = role_of(place)
        place[axes[role]] = (place[axes[role]] + shift) % 4
        place["c"] ^= role ^ role_of(place)
        there = ((place["y"] * 8 + place["z"]) * 4 + place["x"]) * 2 + place["c"]
        pairs.append((i, there))
    return lax.ppermute(block, "rows", pairs)


def ring_scatter(blocks, place):
    own = jnp.where(role_of(place) == 0, *(place[axis] for axis in SECOND_AXIS))
    pick = lambda n: lax.dynamic_index_in_dim(blocks, (own + n) & 3, 0, keepdims=False)
    received = [shifted(pick(n), SECOND_AXIS, n) for n in (1, 3, 2)]
    return (pick(0) + received[0]) + (received[1] + received[2])


def ring_gather(block, place):
    own = jnp.where(role_of(place) == 0, *(place[axis] for axis in SECOND_AXIS))
    received = [(n, shifted(block, SECOND_AXIS, -n)) for n in (1, 3, 2)]
    blocks = jnp.zeros((4, *block.shape), F32)
    for n, part in [(0, block)] + received:
        blocks = lax.dynamic_update_index_in_dim(blocks, part, (own + n) & 3, 0)
    return blocks


def halve(block, place, axes, bit):
    low, high = jnp.split(block, 2)
    upper = (gray_of(place, role_of(place), axes) >> bit) & 1
    sent = exchange(jnp.where(upper == 0, high, low), axes, bit)
    return jnp.where(upper == 0, low, high) + sent


def double(block, place, axes, bit):
    upper = (gray_of(place, role_of(place), axes) >> bit) & 1
    other = exchange(block, axes, bit)
    return jnp.concatenate([jnp.where(upper == 0, block, other), jnp.where(upper == 0, other, block)])


def inner_sum(block, place):
    block = ring_scatter(block, place)
    block = halve(block, place, Z_AXIS, 0)
    for bit in (1, 2):
        block = block + exchange(block, Z_AXIS, bit)
    return ring_gather(double(block, place, Z_AXIS, 0), place)


def order(place, half, stream):
    role = role_of(place) ^ half
    code = gray_of(place, role, FIRST_AXIS)
    first, second = STREAM_BITS[stream]
    return role, (((code >> first) & 1) << 2) | (((code >> second) & 1) << 1)


def cross_blocks(id_ref, features, sketches, outs):
    place = coordinates(id_ref[0])

    @pl.loop(0, outs[0][1].shape[0] // 2)
    def _(pair):
        for (half, stream, start), out in outs:
            role, mask = order(place, half, stream)
            there = (role << 4) | (stream << 3) | ((start + 2 * pair) ^ mask)
            columns = features[:, pl.ds(pl.multiple_of(there * LANES, 256), 256)]
            both = jnp.dot(sketches[...], columns, preferred_element_type=F32)
            cross = both[:SKETCH] + both[SKETCH:]
            out[2 * pair] = cross[:, :LANES]
            out[2 * pair + 1] = cross[:, LANES:]


def send_kernel(id_ref, features_hbm, matrix_hbm, sketches, send0, send1, features, matrix, sems):
    chunks = sems.shape[1]
    width = features.shape[1] // chunks
    copies = []
    for n in range(chunks):
        columns = slice(n * width, (n + 1) * width)
        pair = [
            pltpu.make_async_copy(source.at[:, columns], target.at[:, columns], sems.at[m, n])
            for m, (source, target) in enumerate(((matrix_hbm, matrix), (features_hbm, features)))
        ]
        for copy in pair:
            copy.start()
        copies.append((columns, pair))
    sketch_t = jnp.zeros((SKETCH, features.shape[0]), F32)
    for columns, pair in copies:
        for copy in pair:
            copy.wait()
        sketch_t += dot_nt(matrix[:, columns], features[:, columns])
    high, low = split(sketch_t, 2)
    sketches[:SKETCH, :] = high
    sketches[SKETCH:, :] = low
    cross_blocks(id_ref, features, sketches, (((1, 0, 0), send0), ((1, 1, 0), send1)))


def keep_kernel(id_ref, features, sketches, low0, high0, low1, high1):
    wanted = ((0, 0, 0), (0, 0, 4), (0, 1, 0), (0, 1, 4))
    cross_blocks(id_ref, features, sketches, tuple(zip(wanted, (low0, high0, low1, high1))))


def call(kernel, operands, outs, scratch=(), flops=0, limit=24, space=pltpu.VMEM):
    vmem = pl.BlockSpec(memory_space=pltpu.VMEM)
    return pl.pallas_call(
        kernel,
        out_shape=[jax.ShapeDtypeStruct(shape, dtype) for shape, dtype in outs],
        in_specs=[pl.BlockSpec(memory_space=pltpu.SMEM)]
        + [pl.BlockSpec(memory_space=space)] * (len(operands) - 1),
        out_specs=[vmem] * len(outs),
        scratch_shapes=scratch,
        compiler_params=pltpu.CompilerParams(vmem_limit_bytes=limit * 1024 * 1024),
        cost_estimate=pl.CostEstimate(flops=flops, bytes_accessed=4 * 1024 * 1024, transcendentals=0),
    )(*operands)


def scatter_stream(stream, low, high, received):
    first, second = STREAM_BITS[stream]
    back = exchange(high + received[4:], FIRST_AXIS, first)
    block = low + received[:4]
    back_next = exchange(block[2:] + back[2:], FIRST_AXIS, second)
    return block[:2] + back[:2] + back_next


def split(value, terms):
    parts = []
    for _ in range(terms):
        part = value.astype(BF16)
        parts.append(part)
        value = value - part.astype(F32)
    return parts


def dot_nt(a, b, precision=None):
    return lax.dot_general(
        a, b, (((1,), (1,)), ((), ())), precision=precision, preferred_element_type=F32
    )


def dot(a, b, precision=None):
    return jnp.dot(a, b, precision=precision, preferred_element_type=F32)


def dot_three(a, b):
    a0, a1 = split(a, 2)
    b0, b1 = split(b, 2)
    return dot(a0, b0) + (dot(a0, b1) + dot(a1, b0))


def stacked(rows, terms):
    parts = split(rows, 3)
    return jnp.concatenate([parts[n] for n in terms], axis=0)


def beside(value):
    lane = lax.broadcasted_iota(jnp.int32, value.shape, 1)
    parts = [part.astype(F32) for part in split(value, 3)]
    turned = [pltpu.roll(part, BLOCK, 1) for part in parts[:2]]
    pairs = ((0, 0), (1, 0), (2, 1))
    return jnp.concatenate(
        [jnp.where(lane < BLOCK, parts[m], turned[n]).astype(BF16) for m, n in pairs], axis=1
    )


UNDER = (0, 1, 0, 2, 0, 1)


def factor_blocks(blocks, outs, meanwhile):
    groups = BLOCK // 8
    lane = lax.broadcasted_iota(jnp.int32, (8, LANES), 1)
    sub = lax.broadcasted_iota(jnp.int32, (8, LANES), 0)
    work = []
    for block in blocks:
        rows = []
        for g in range(groups):
            unit = jnp.where(lane - BLOCK == sub + 8 * g, 1.0, 0.0).astype(F32)
            rows.append(jnp.where(lane < BLOCK, block[8 * g : 8 * g + 8], unit))
        work.append(rows)
    for g in range(groups):
        columns = [
            [
                [
                    jnp.broadcast_to(rows[r][:, 8 * g + j : 8 * g + j + 1], (8, LANES))
                    for r in range(g, groups)
                ]
                for j in range(8)
            ]
            for rows in work
        ]
        for k in range(8):
            for rows, cols, out in zip(work, columns, outs):
                pivot = cols[k][0][k : k + 1, :]
                inverse = 1.0 / pivot
                row = rows[g][k : k + 1, :]
                out[8 * g + k : 8 * g + k + 1, :] = row * lax.rsqrt(pivot)
                scaled = row * inverse
                for j in range(k + 1, 8):
                    factor = cols[j][0][k : k + 1, :] * inverse
                    for r in range(groups - g):
                        cols[j][r] = cols[j][r] - cols[k][r] * factor
                for r in range(g, groups):
                    column = cols[k][r - g]
                    if r == g:
                        column = jnp.where(sub > k, column, 0.0)
                    rows[r] = rows[r] - column * scaled
        if meanwhile:
            meanwhile.pop(0)()


def factor_all(mats, outs, upper):
    column = lax.broadcasted_iota(jnp.int32, (BLOCK, PAD), 1)
    row = lax.broadcasted_iota(jnp.int32, (BLOCK, PAD), 0)
    lane = lax.broadcasted_iota(jnp.int32, (BLOCK, LANES), 1)
    line = lax.broadcasted_iota(jnp.int32, (BLOCK, LANES), 0)
    steps = SKETCH // BLOCK
    meanwhile = []

    def update(mat, change, step, first, last):
        rows = slice(first * BLOCK, last * BLOCK)
        keep = lax.broadcasted_iota(jnp.int32, ((last - first) * BLOCK, PAD), 1)
        keep = (keep < step * BLOCK) | (keep >= (step + 1) * BLOCK)
        mat[rows, :] = jnp.where(keep, mat[rows, :], 0.0) - change

    for step in range(steps):
        here = slice(step * BLOCK, (step + 1) * BLOCK)
        window = slice(step // 2 * LANES, (step // 2 + 1) * LANES)
        odd = step % 2 == 1
        blocks = []
        for mat in mats:
            block = mat[here, window]
            blocks.append(pltpu.roll(block, BLOCK, 1) if odd else block)
        factor_blocks(blocks, outs, meanwhile)
        inside = (column >= step * BLOCK) & (column < (step + 1) * BLOCK)
        for n, (mat, out) in enumerate(zip(mats, outs)):
            both = out[...]
            inverse = beside(pltpu.roll(both, BLOCK, 1))
            line_up = jnp.where(inside, jnp.where(column - step * BLOCK == row, 1.0, 0.0), mat[here, :])
            panel = dot(inverse, stacked(line_up, UNDER))
            mat[here, :] = panel
            if n == 0:
                upper[here, :] = jnp.where(column >= (step + 1) * BLOCK, panel, 0.0)
                corner = jnp.where((lane < BLOCK) & (lane >= line), both, 0.0)
                corner = pltpu.roll(corner, BLOCK, 1) if odd else corner
                upper[here, window] = upper[here, window] + corner
            if step == steps - 1:
                continue
            start = (step + 1) * BLOCK // LANES * LANES
            turned = jnp.transpose(panel[:, start:])
            turned = jnp.concatenate([turned, jnp.zeros_like(turned)], axis=1)
            left, right = beside(turned), stacked(panel, UNDER)
            skip = (step + 1) * BLOCK - start
            update(mat, dot(left[skip : skip + BLOCK], right), step, step + 1, step + 2)
            if step < steps - 2:

                def rest(mat=mat, left=left, right=right, step=step, skip=skip):
                    stop = SKETCH - start_of(step)
                    update(mat, dot(left[skip + BLOCK : stop], right), step, step + 2, steps)

                def start_of(step):
                    return (step + 1) * BLOCK // LANES * LANES

                meanwhile.append(rest)


def columns_of(place, half, part, stream):
    role, mask = order(place, half, stream)
    first = (role << 4) | (stream << 3) | ((4 * part) ^ (mask & 4))
    return pl.ds(pl.multiple_of(first * LANES, WIDTH), WIDTH)


def pieces_kernel(member, id_ref, sketch_matrix_t, piece, *refs):
    before, (terms, sums, left, right, cross, mix) = refs[:-6], refs[-6:]
    place = coordinates(id_ref[0])
    _, mask = order(place, member[0], member[2])
    for slot in range(4):
        start = (slot ^ (mask & 2)) * LANES
        cross[:, pl.ds(pl.multiple_of(start, LANES), LANES)] = piece[slot]
    a, b, c = split(cross[...], 3)
    for n, (term, again) in enumerate(((a, a), (b, b), (c, a))):
        left[n * SKETCH : (n + 1) * SKETCH, :] = term
        terms[n * SKETCH : (n + 1) * SKETCH, :] = again
    right[:SKETCH, :] = a
    right[SKETCH:PAD, :] = jnp.zeros((PAD - SKETCH, WIDTH), BF16)
    right[PAD:, :] = sketch_matrix_t[:, columns_of(place, *member)]
    both = dot_nt(left[...], right[...])
    parts = [both[n * SKETCH : (n + 1) * SKETCH] for n in range(3)]
    mix[...] = jnp.zeros_like(mix)
    mix[:SKETCH, :SKETCH] = parts[1][:, :SKETCH] + parts[2][:, :SKETCH]
    mixed = (mix[...] + jnp.transpose(mix[...]))[:SKETCH]
    sums[...] = before[0][...] if before else jnp.zeros_like(sums)
    sums[0, :, :SKETCH] += parts[0][:, PAD:] + (parts[1][:, PAD:] + parts[2][:, PAD:])
    sums[1, :, :SKETCH] += parts[0][:, :SKETCH] + dot_nt(b, b)
    sums[1] += mixed


def factor_kernel(scale, id_ref, own, other, basis_map, inverse_c, gram, coupling, upper, out0, out1, wide):
    for n, ref in enumerate((gram, coupling)):
        ref[...] = jnp.zeros_like(ref)
        ref[:SKETCH, :] = own[n] + other[n]
    upper[...] = jnp.zeros_like(upper)
    factor_all((gram, coupling), (out0, out1), upper)
    row = lax.broadcasted_iota(jnp.int32, (PAD, PAD), 0)
    column = lax.broadcasted_iota(jnp.int32, (PAD, PAD), 1)
    lower = (row < SKETCH) & (column <= row)
    high, low = split(jnp.where(lower, gram[...], 0.0)[:SKETCH, :SKETCH], 2)
    for n, term in enumerate((high, high, low)):
        wide[:, n * SKETCH : (n + 1) * SKETCH] = term.astype(F32)
    basis_map[...] = wide[...].astype(BF16)
    chain = dot_three(jnp.where(lower, coupling[...], 0.0), jnp.transpose(upper[...]))
    gram[...] = dot_three(jnp.transpose(chain), chain) * scale
    inverse_c[...] = gram[:SKETCH, :SKETCH]


def final_kernel(members, id_ref, features, basis_map, inverse_c, *refs):
    terms, (result, coeffs) = refs[:-2], refs[-2:]
    place = coordinates(id_ref[0])
    part = WIDTH // 2

    @pl.loop(0, 2)
    def _(n):
        here = pl.ds(pl.multiple_of(n * part, part), part)
        for term, member in zip(terms, members):
            start = pl.multiple_of(columns_of(place, *member).start + n * part, part)
            coeffs[:, pl.ds(start, part)] = dot(basis_map[...], term[:, here]).astype(BF16)

    projected = dot_nt(coeffs[...], features[...])
    result[...] = dot_three(inverse_c[...], projected)


def body(features, sketch_matrix):
    rows, width = features.shape
    rows_total = rows * lax.axis_size("rows")
    device = lax.axis_index("rows").astype(jnp.int32)[None]
    whole, piece = ((8, SKETCH, LANES), F32), ((4, SKETCH, LANES), F32)
    flops = 2 * rows * width * SKETCH

    sketch_matrix_t = sketch_matrix.T

    sketches, send0, send1 = call(
        send_kernel,
        (device, features, sketch_matrix_t),
        [((2 * SKETCH, rows), BF16), whole, whole],
        scratch=[
            pltpu.VMEM((rows, width), BF16),
            pltpu.VMEM((SKETCH, width), BF16),
            pltpu.SemaphoreType.DMA((2, 4)),
        ],
        flops=2 * flops,
        space=pltpu.HBM,
        limit=50,
    )
    received = across(send0), across(send1)
    low0, high0, low1, high1 = call(
        keep_kernel, (device, features, sketches), [piece] * 4, flops=flops
    )
    block = jnp.concatenate(
        [scatter_stream(0, low0, high0, received[0]), scatter_stream(1, low1, high1, received[1])]
    )
    block = inner_sum(block, coordinates(device[0]))
    streams = []
    for stream, (first, second) in enumerate(STREAM_BITS):
        own = block[2 * stream : 2 * stream + 2]
        own = jnp.concatenate([own, exchange(own, FIRST_AXIS, second)])
        streams.append((own, exchange(own, FIRST_AXIS, first)))

    members = [(0, part, stream) for part in range(2) for stream in range(2)]
    terms_shape = ((3 * SKETCH, WIDTH), BF16)
    sums_shape = ((2, SKETCH, PAD), F32)
    terms, sums = [], ()
    for member in members:
        _, part, stream = member
        term, *sums = call(
            functools.partial(pieces_kernel, member),
            (device, sketch_matrix_t, streams[stream][part], *sums),
            [terms_shape, sums_shape],
            scratch=[
                pltpu.VMEM(*terms_shape),
                pltpu.VMEM((PAD + SKETCH, WIDTH), BF16),
                pltpu.VMEM((SKETCH, WIDTH), F32),
                pltpu.VMEM((PAD, PAD), F32),
            ],
        )
        terms.append(term)
    square, corner = pltpu.VMEM((PAD, PAD), F32), pltpu.VMEM((BLOCK, LANES), F32)
    basis_map, inverse_c = call(
        functools.partial(factor_kernel, math.sqrt(rows_total)),
        (device, *sums, across(*sums)),
        [((SKETCH, 3 * SKETCH), BF16), ((SKETCH, SKETCH), F32)],
        scratch=[square] * 3 + [corner] * 2 + [pltpu.VMEM((SKETCH, 3 * SKETCH), F32)],
        flops=14 * flops,
    )
    terms += [across(term) for term in terms]
    members += [(1, part, stream) for _, part, stream in members]
    (result,) = call(
        functools.partial(final_kernel, members),
        (device, features, basis_map, inverse_c, *terms),
        [((SKETCH, rows), F32)],
        scratch=[pltpu.VMEM((SKETCH, width), BF16)],
        flops=4 * flops,
    )
    return result.T


def solution(mesh):
    return jax.shard_map(
        body,
        mesh=mesh,
        in_specs=(P("rows", None), P()),
        out_specs=P("rows", None),
        check_vma=False,
    )
```

```python
import functools
import math

import jax
import jax.numpy as jnp
from jax import lax
from jax.experimental import pallas as pl
from jax.experimental.pallas import tpu as pltpu
from jax.sharding import PartitionSpec as P

SKETCH = 320
PAD = 384
BLOCK = 64
LANES = 128
WIDTH = 4 * LANES
F32 = jnp.float32
BF16 = jnp.bfloat16

FIRST_AXIS = ("y", "x")
SECOND_AXIS = ("x", "y")
Z_AXIS = ("z", "z")
STREAM_BITS = ((0, 1), (1, 0))


def coordinates(index):
    return {"c": index & 1, "x": (index >> 1) & 3, "z": (index >> 3) & 7, "y": (index >> 6) & 3}


def role_of(place):
    return place["c"] ^ ((place["x"] + place["y"] + place["z"]) & 1)


def gray(value):
    return value ^ (value >> 1)


def gray_of(place, role, axes):
    return jnp.where(role == 0, *(gray(place[axis]) for axis in axes))


def across(block):
    return lax.ppermute(block, "rows", [(i, i ^ 1) for i in range(lax.axis_size("rows"))])


def exchange(block, axes, bits):
    pairs = []
    for i in range(lax.axis_size("rows")):
        place = coordinates(i)
        role = role_of(place)
        wanted = gray(place[axes[role]]) ^ bits
        place[axes[role]] = next(v for v in range(8) if gray(v) == wanted)
        place["c"] ^= role ^ role_of(place)
        there = ((place["y"] * 8 + place["z"]) * 4 + place["x"]) * 2 + place["c"]
        pairs.append((i, there))
    return lax.ppermute(block, "rows", pairs)


def shifted(block, axes, shift):
    pairs = []
    for i in range(lax.axis_size("rows")):
        place = coordinates(i)
        role = role_of(place)
        place[axes[role]] = (place[axes[role]] + shift) % 4
        place["c"] ^= role ^ role_of(place)
        there = ((place["y"] * 8 + place["z"]) * 4 + place["x"]) * 2 + place["c"]
        pairs.append((i, there))
    return lax.ppermute(block, "rows", pairs)


def ring_scatter(blocks, place):
    own = jnp.where(role_of(place) == 0, *(place[axis] for axis in SECOND_AXIS))
    pick = lambda n: lax.dynamic_index_in_dim(blocks, (own + n) & 3, 0, keepdims=False)
    received = [shifted(pick(n), SECOND_AXIS, n) for n in (1, 3, 2)]
    return (pick(0) + received[0]) + (received[1] + received[2])


def ring_gather(block, place):
    own = jnp.where(role_of(place) == 0, *(place[axis] for axis in SECOND_AXIS))
    received = [(n, shifted(block, SECOND_AXIS, -n)) for n in (1, 3, 2)]
    blocks = jnp.zeros((4, *block.shape), F32)
    for n, part in [(0, block)] + received:
        blocks = lax.dynamic_update_index_in_dim(blocks, part, (own + n) & 3, 0)
    return blocks


def halve(block, place, axes, bit):
    low, high = jnp.split(block, 2)
    upper = (gray_of(place, role_of(place), axes) >> bit) & 1
    sent = exchange(jnp.where(upper == 0, high, low), axes, 1 << bit)
    return jnp.where(upper == 0, low, high) + sent


def double(block, place, axes, bit):
    upper = (gray_of(place, role_of(place), axes) >> bit) & 1
    other = exchange(block, axes, 1 << bit)
    return jnp.concatenate([jnp.where(upper == 0, block, other), jnp.where(upper == 0, other, block)])


def inner_sum(block, place):
    block = ring_scatter(block, place)
    block = halve(block, place, Z_AXIS, 0)
    others = [exchange(block, Z_AXIS, bits) for bits in (2, 4, 6)]
    block = (block + others[0]) + (others[1] + others[2])
    return ring_gather(double(block, place, Z_AXIS, 0), place)


def order(place, half, stream):
    role = role_of(place) ^ half
    code = gray_of(place, role, FIRST_AXIS)
    first, second = STREAM_BITS[stream]
    return role, (((code >> first) & 1) << 2) | (((code >> second) & 1) << 1)


def cross_blocks(id_ref, features, sketches, outs):
    place = coordinates(id_ref[0])

    @pl.loop(0, outs[0][1].shape[0] // 2)
    def _(pair):
        for (half, stream, start), out in outs:
            role, mask = order(place, half, stream)
            there = (role << 4) | (stream << 3) | ((start + 2 * pair) ^ mask)
            columns = features[:, pl.ds(pl.multiple_of(there * LANES, 256), 256)]
            both = jnp.dot(sketches[...], columns, preferred_element_type=F32)
            cross = both[:SKETCH] + both[SKETCH:]
            out[2 * pair] = cross[:, :LANES]
            out[2 * pair + 1] = cross[:, LANES:]


def send_kernel(id_ref, features_hbm, matrix_hbm, sketches, send0, send1, features, matrix, sems):
    chunks = sems.shape[1]
    width = features.shape[1] // chunks
    copies = []
    for n in range(chunks):
        columns = slice(n * width, (n + 1) * width)
        pair = [
            pltpu.make_async_copy(source.at[:, columns], target.at[:, columns], sems.at[m, n])
            for m, (source, target) in enumerate(((matrix_hbm, matrix), (features_hbm, features)))
        ]
        for copy in pair:
            copy.start()
        copies.append((columns, pair))
    sketch_t = jnp.zeros((SKETCH, features.shape[0]), F32)
    for columns, pair in copies:
        for copy in pair:
            copy.wait()
        sketch_t += dot_nt(matrix[:, columns], features[:, columns])
    high, low = split(sketch_t, 2)
    sketches[:SKETCH, :] = high
    sketches[SKETCH:, :] = low
    cross_blocks(id_ref, features, sketches, (((1, 0, 0), send0), ((1, 1, 0), send1)))


def keep_kernel(id_ref, features, sketches, low0, high0, low1, high1):
    wanted = ((0, 0, 0), (0, 0, 4), (0, 1, 0), (0, 1, 4))
    cross_blocks(id_ref, features, sketches, tuple(zip(wanted, (low0, high0, low1, high1))))


def call(kernel, operands, outs, scratch=(), flops=0, limit=24, space=pltpu.VMEM):
    vmem = pl.BlockSpec(memory_space=pltpu.VMEM)
    return pl.pallas_call(
        kernel,
        out_shape=[jax.ShapeDtypeStruct(shape, dtype) for shape, dtype in outs],
        in_specs=[pl.BlockSpec(memory_space=pltpu.SMEM)]
        + [pl.BlockSpec(memory_space=space)] * (len(operands) - 1),
        out_specs=[vmem] * len(outs),
        scratch_shapes=scratch,
        compiler_params=pltpu.CompilerParams(vmem_limit_bytes=limit * 1024 * 1024),
        cost_estimate=pl.CostEstimate(flops=flops, bytes_accessed=4 * 1024 * 1024, transcendentals=0),
    )(*operands)


def scatter_stream(stream, low, high, received):
    first, second = STREAM_BITS[stream]
    back = exchange(high + received[4:], FIRST_AXIS, 1 << first)
    block = low + received[:4]
    back_next = exchange(block[2:] + back[2:], FIRST_AXIS, 1 << second)
    return block[:2] + back[:2] + back_next


def split(value, terms):
    parts = []
    for _ in range(terms):
        part = value.astype(BF16)
        parts.append(part)
        value = value - part.astype(F32)
    return parts


def dot_nt(a, b, precision=None):
    return lax.dot_general(
        a, b, (((1,), (1,)), ((), ())), precision=precision, preferred_element_type=F32
    )


def dot(a, b, precision=None):
    return jnp.dot(a, b, precision=precision, preferred_element_type=F32)


def dot_three(a, b):
    a0, a1 = split(a, 2)
    b0, b1 = split(b, 2)
    return dot(a0, b0) + (dot(a0, b1) + dot(a1, b0))


def stacked(rows, terms):
    parts = split(rows, 3)
    return jnp.concatenate([parts[n] for n in terms], axis=0)


def beside(value):
    lane = lax.broadcasted_iota(jnp.int32, value.shape, 1)
    parts = [part.astype(F32) for part in split(value, 3)]
    turned = [pltpu.roll(part, BLOCK, 1) for part in parts[:2]]
    pairs = ((0, 0), (1, 0), (2, 1))
    return jnp.concatenate(
        [jnp.where(lane < BLOCK, parts[m], turned[n]).astype(BF16) for m, n in pairs], axis=1
    )


UNDER = (0, 1, 0, 2, 0, 1)


def factor_blocks(blocks, outs, meanwhile):
    groups = BLOCK // 8
    lane = lax.broadcasted_iota(jnp.int32, (8, LANES), 1)
    sub = lax.broadcasted_iota(jnp.int32, (8, LANES), 0)
    work = []
    for block in blocks:
        rows = []
        for g in range(groups):
            unit = jnp.where(lane - BLOCK == sub + 8 * g, 1.0, 0.0).astype(F32)
            rows.append(jnp.where(lane < BLOCK, block[8 * g : 8 * g + 8], unit))
        work.append(rows)
    for g in range(groups):
        columns = [
            [
                [
                    jnp.broadcast_to(rows[r][:, 8 * g + j : 8 * g + j + 1], (8, LANES))
                    for r in range(g, groups)
                ]
                for j in range(8)
            ]
            for rows in work
        ]
        for k in range(8):
            for rows, cols, out in zip(work, columns, outs):
                pivot = cols[k][0][k : k + 1, :]
                inverse = 1.0 / pivot
                row = rows[g][k : k + 1, :]
                out[8 * g + k : 8 * g + k + 1, :] = row * lax.rsqrt(pivot)
                scaled = row * inverse
                for j in range(k + 1, 8):
                    factor = cols[j][0][k : k + 1, :] * inverse
                    for r in range(groups - g):
                        cols[j][r] = cols[j][r] - cols[k][r] * factor
                for r in range(g, groups):
                    column = cols[k][r - g]
                    if r == g:
                        column = jnp.where(sub > k, column, 0.0)
                    rows[r] = rows[r] - column * scaled
        if meanwhile:
            meanwhile.pop(0)()


def factor_all(mats, outs, upper):
    column = lax.broadcasted_iota(jnp.int32, (BLOCK, PAD), 1)
    row = lax.broadcasted_iota(jnp.int32, (BLOCK, PAD), 0)
    lane = lax.broadcasted_iota(jnp.int32, (BLOCK, LANES), 1)
    line = lax.broadcasted_iota(jnp.int32, (BLOCK, LANES), 0)
    steps = SKETCH // BLOCK
    meanwhile = []

    def update(mat, change, step, first, last):
        rows = slice(first * BLOCK, last * BLOCK)
        keep = lax.broadcasted_iota(jnp.int32, ((last - first) * BLOCK, PAD), 1)
        keep = (keep < step * BLOCK) | (keep >= (step + 1) * BLOCK)
        mat[rows, :] = jnp.where(keep, mat[rows, :], 0.0) - change

    for step in range(steps):
        here = slice(step * BLOCK, (step + 1) * BLOCK)
        window = slice(step // 2 * LANES, (step // 2 + 1) * LANES)
        odd = step % 2 == 1
        blocks = []
        for mat in mats:
            block = mat[here, window]
            blocks.append(pltpu.roll(block, BLOCK, 1) if odd else block)
        factor_blocks(blocks, outs, meanwhile)
        inside = (column >= step * BLOCK) & (column < (step + 1) * BLOCK)
        for n, (mat, out) in enumerate(zip(mats, outs)):
            both = out[...]
            inverse = beside(pltpu.roll(both, BLOCK, 1))
            line_up = jnp.where(inside, jnp.where(column - step * BLOCK == row, 1.0, 0.0), mat[here, :])
            panel = dot(inverse, stacked(line_up, UNDER))
            mat[here, :] = panel
            if n == 0:
                upper[here, :] = jnp.where(column >= (step + 1) * BLOCK, panel, 0.0)
                corner = jnp.where((lane < BLOCK) & (lane >= line), both, 0.0)
                corner = pltpu.roll(corner, BLOCK, 1) if odd else corner
                upper[here, window] = upper[here, window] + corner
            if step == steps - 1:
                continue
            start = (step + 1) * BLOCK // LANES * LANES
            turned = jnp.transpose(panel[:, start:])
            turned = jnp.concatenate([turned, jnp.zeros_like(turned)], axis=1)
            left, right = beside(turned), stacked(panel, UNDER)
            skip = (step + 1) * BLOCK - start
            update(mat, dot(left[skip : skip + BLOCK], right), step, step + 1, step + 2)
            if step < steps - 2:

                def rest(mat=mat, left=left, right=right, step=step, skip=skip):
                    stop = SKETCH - start_of(step)
                    update(mat, dot(left[skip + BLOCK : stop], right), step, step + 2, steps)

                def start_of(step):
                    return (step + 1) * BLOCK // LANES * LANES

                meanwhile.append(rest)


def columns_of(place, half, part, stream):
    role, mask = order(place, half, stream)
    first = (role << 4) | (stream << 3) | ((4 * part) ^ (mask & 4))
    return pl.ds(pl.multiple_of(first * LANES, WIDTH), WIDTH)


def pieces_kernel(member, id_ref, sketch_matrix_t, piece, *refs):
    before, (terms, sums, left, right, cross, mix) = refs[:-6], refs[-6:]
    place = coordinates(id_ref[0])
    _, mask = order(place, member[0], member[2])
    for slot in range(4):
        start = (slot ^ (mask & 2)) * LANES
        cross[:, pl.ds(pl.multiple_of(start, LANES), LANES)] = piece[slot]
    a, b, c = split(cross[...], 3)
    for n, (term, again) in enumerate(((a, a), (b, b), (c, a))):
        left[n * SKETCH : (n + 1) * SKETCH, :] = term
        terms[n * SKETCH : (n + 1) * SKETCH, :] = again
    right[:SKETCH, :] = a
    right[SKETCH:PAD, :] = jnp.zeros((PAD - SKETCH, WIDTH), BF16)
    right[PAD:, :] = sketch_matrix_t[:, columns_of(place, *member)]
    both = dot_nt(left[...], right[...])
    parts = [both[n * SKETCH : (n + 1) * SKETCH] for n in range(3)]
    mix[...] = jnp.zeros_like(mix)
    mix[:SKETCH, :SKETCH] = parts[1][:, :SKETCH] + parts[2][:, :SKETCH]
    mixed = (mix[...] + jnp.transpose(mix[...]))[:SKETCH]
    sums[...] = before[0][...] if before else jnp.zeros_like(sums)
    sums[0, :, :SKETCH] += parts[0][:, PAD:] + (parts[1][:, PAD:] + parts[2][:, PAD:])
    sums[1, :, :SKETCH] += parts[0][:, :SKETCH] + dot_nt(b, b)
    sums[1] += mixed


def factor_kernel(scale, id_ref, own, other, basis_map, inverse_c, gram, coupling, upper, out0, out1, wide):
    for n, ref in enumerate((gram, coupling)):
        ref[...] = jnp.zeros_like(ref)
        ref[:SKETCH, :] = own[n] + other[n]
    upper[...] = jnp.zeros_like(upper)
    factor_all((gram, coupling), (out0, out1), upper)
    row = lax.broadcasted_iota(jnp.int32, (PAD, PAD), 0)
    column = lax.broadcasted_iota(jnp.int32, (PAD, PAD), 1)
    lower = (row < SKETCH) & (column <= row)
    high, low = split(jnp.where(lower, gram[...], 0.0)[:SKETCH, :SKETCH], 2)
    for n, term in enumerate((high, high, low)):
        wide[:, n * SKETCH : (n + 1) * SKETCH] = term.astype(F32)
    basis_map[...] = wide[...].astype(BF16)
    chain = dot_three(jnp.where(lower, coupling[...], 0.0), jnp.transpose(upper[...]))
    gram[...] = dot_three(jnp.transpose(chain), chain) * scale
    inverse_c[...] = gram[:SKETCH, :SKETCH]


def final_kernel(members, id_ref, features, basis_map, inverse_c, *refs):
    terms, (result, coeffs) = refs[:-2], refs[-2:]
    place = coordinates(id_ref[0])
    part = WIDTH // 2

    @pl.loop(0, 2)
    def _(n):
        here = pl.ds(pl.multiple_of(n * part, part), part)
        for term, member in zip(terms, members):
            start = pl.multiple_of(columns_of(place, *member).start + n * part, part)
            coeffs[:, pl.ds(start, part)] = dot(basis_map[...], term[:, here]).astype(BF16)

    projected = dot_nt(coeffs[...], features[...])
    result[...] = dot_three(inverse_c[...], projected)


def body(features, sketch_matrix):
    rows, width = features.shape
    rows_total = rows * lax.axis_size("rows")
    device = lax.axis_index("rows").astype(jnp.int32)[None]
    whole, piece = ((8, SKETCH, LANES), F32), ((4, SKETCH, LANES), F32)
    flops = 2 * rows * width * SKETCH

    sketch_matrix_t = sketch_matrix.T

    sketches, send0, send1 = call(
        send_kernel,
        (device, features, sketch_matrix_t),
        [((2 * SKETCH, rows), BF16), whole, whole],
        scratch=[
            pltpu.VMEM((rows, width), BF16),
            pltpu.VMEM((SKETCH, width), BF16),
            pltpu.SemaphoreType.DMA((2, 4)),
        ],
        flops=2 * flops,
        space=pltpu.HBM,
        limit=50,
    )
    received = across(send0), across(send1)
    low0, high0, low1, high1 = call(
        keep_kernel, (device, features, sketches), [piece] * 4, flops=flops
    )
    block = jnp.concatenate(
        [scatter_stream(0, low0, high0, received[0]), scatter_stream(1, low1, high1, received[1])]
    )
    block = inner_sum(block, coordinates(device[0]))
    streams = []
    for stream, (first, second) in enumerate(STREAM_BITS):
        own = block[2 * stream : 2 * stream + 2]
        own = jnp.concatenate([own, exchange(own, FIRST_AXIS, 1 << second)])
        streams.append((own, exchange(own, FIRST_AXIS, 1 << first)))

    members = [(0, part, stream) for part in range(2) for stream in range(2)]
    terms_shape = ((3 * SKETCH, WIDTH), BF16)
    sums_shape = ((2, SKETCH, PAD), F32)
    terms, sums = [], ()
    for member in members:
        _, part, stream = member
        term, *sums = call(
            functools.partial(pieces_kernel, member),
            (device, sketch_matrix_t, streams[stream][part], *sums),
            [terms_shape, sums_shape],
            scratch=[
                pltpu.VMEM(*terms_shape),
                pltpu.VMEM((PAD + SKETCH, WIDTH), BF16),
                pltpu.VMEM((SKETCH, WIDTH), F32),
                pltpu.VMEM((PAD, PAD), F32),
            ],
        )
        terms.append(term)
    square, corner = pltpu.VMEM((PAD, PAD), F32), pltpu.VMEM((BLOCK, LANES), F32)
    basis_map, inverse_c = call(
        functools.partial(factor_kernel, math.sqrt(rows_total)),
        (device, *sums, across(*sums)),
        [((SKETCH, 3 * SKETCH), BF16), ((SKETCH, SKETCH), F32)],
        scratch=[square] * 3 + [corner] * 2 + [pltpu.VMEM((SKETCH, 3 * SKETCH), F32)],
        flops=14 * flops,
    )
    terms += [across(term) for term in terms]
    members += [(1, part, stream) for _, part, stream in members]
    (result,) = call(
        functools.partial(final_kernel, members),
        (device, features, basis_map, inverse_c, *terms),
        [((SKETCH, rows), F32)],
        scratch=[pltpu.VMEM((SKETCH, width), BF16)],
        flops=4 * flops,
    )
    return result.T


def solution(mesh):
    return jax.shard_map(
        body,
        mesh=mesh,
        in_specs=(P("rows", None), P()),
        out_specs=P("rows", None),
        check_vma=False,
    )
```

```python
import functools
import math

import jax
import jax.numpy as jnp
from jax import lax
from jax.experimental import pallas as pl
from jax.experimental.pallas import tpu as pltpu
from jax.sharding import PartitionSpec as P

SKETCH = 320
PAD = 384
BLOCK = 64
LANES = 128
WIDTH = 4 * LANES
F32 = jnp.float32
BF16 = jnp.bfloat16

FIRST_AXIS = ("y", "x")
SECOND_AXIS = ("x", "y")
Z_AXIS = ("z", "z")
STREAM_BITS = ((0, 1), (1, 0))


def coordinates(index):
    return {"c": index & 1, "x": (index >> 1) & 3, "z": (index >> 3) & 7, "y": (index >> 6) & 3}


def role_of(place):
    return place["c"] ^ ((place["x"] + place["y"] + place["z"]) & 1)


def gray(value):
    return value ^ (value >> 1)


def gray_of(place, role, axes):
    return jnp.where(role == 0, *(gray(place[axis]) for axis in axes))


def across(block):
    return lax.ppermute(block, "rows", [(i, i ^ 1) for i in range(lax.axis_size("rows"))])


def exchange(block, axes, bits):
    pairs = []
    for i in range(lax.axis_size("rows")):
        place = coordinates(i)
        role = role_of(place)
        wanted = gray(place[axes[role]]) ^ bits
        place[axes[role]] = next(v for v in range(8) if gray(v) == wanted)
        place["c"] ^= role ^ role_of(place)
        there = ((place["y"] * 8 + place["z"]) * 4 + place["x"]) * 2 + place["c"]
        pairs.append((i, there))
    return lax.ppermute(block, "rows", pairs)


def shifted(block, axes, shift):
    pairs = []
    for i in range(lax.axis_size("rows")):
        place = coordinates(i)
        role = role_of(place)
        place[axes[role]] = (place[axes[role]] + shift) % 4
        place["c"] ^= role ^ role_of(place)
        there = ((place["y"] * 8 + place["z"]) * 4 + place["x"]) * 2 + place["c"]
        pairs.append((i, there))
    return lax.ppermute(block, "rows", pairs)


def ring_scatter(blocks, place):
    own = jnp.where(role_of(place) == 0, *(place[axis] for axis in SECOND_AXIS))
    pick = lambda n: lax.dynamic_index_in_dim(blocks, (own + n) & 3, 0, keepdims=False)
    received = [shifted(pick(n), SECOND_AXIS, n) for n in (1, 3, 2)]
    return (pick(0) + received[0]) + (received[1] + received[2])


def ring_gather(block, place):
    own = jnp.where(role_of(place) == 0, *(place[axis] for axis in SECOND_AXIS))
    received = [(n, shifted(block, SECOND_AXIS, -n)) for n in (1, 3, 2)]
    blocks = jnp.zeros((4, *block.shape), F32)
    for n, part in [(0, block)] + received:
        blocks = lax.dynamic_update_index_in_dim(blocks, part, (own + n) & 3, 0)
    return blocks


def halve(block, place, axes, bit):
    low, high = jnp.split(block, 2)
    upper = (gray_of(place, role_of(place), axes) >> bit) & 1
    sent = exchange(jnp.where(upper == 0, high, low), axes, 1 << bit)
    return jnp.where(upper == 0, low, high) + sent


def double(block, place, axes, bit):
    upper = (gray_of(place, role_of(place), axes) >> bit) & 1
    other = exchange(block, axes, 1 << bit)
    return jnp.concatenate([jnp.where(upper == 0, block, other), jnp.where(upper == 0, other, block)])


def inner_sum(block, place):
    block = ring_scatter(block, place)
    block = halve(block, place, Z_AXIS, 0)
    others = [exchange(block, Z_AXIS, bits) for bits in (2, 4, 6)]
    block = (block + others[0]) + (others[1] + others[2])
    return ring_gather(double(block, place, Z_AXIS, 0), place)


def order(place, half, stream):
    role = role_of(place) ^ half
    code = gray_of(place, role, FIRST_AXIS)
    first, second = STREAM_BITS[stream]
    return role, (((code >> first) & 1) << 2) | (((code >> second) & 1) << 1)


def cross_blocks(id_ref, features, sketches, outs):
    place = coordinates(id_ref[0])

    @pl.loop(0, outs[0][1].shape[0] // 2)
    def _(pair):
        for (half, stream, start), out in outs:
            role, mask = order(place, half, stream)
            there = (role << 4) | (stream << 3) | ((start + 2 * pair) ^ mask)
            columns = features[:, pl.ds(pl.multiple_of(there * LANES, 256), 256)]
            both = jnp.dot(sketches[...], columns, preferred_element_type=F32)
            cross = both[:SKETCH] + both[SKETCH:]
            out[2 * pair] = cross[:, :LANES]
            out[2 * pair + 1] = cross[:, LANES:]


def send_kernel(id_ref, features_hbm, matrix_hbm, sketches, send0, send1, features, matrix, total, sems):
    chunks = sems.shape[1]
    width = features.shape[1] // chunks

    def copies(n):
        columns = pl.ds(pl.multiple_of(n * width, width), width)
        return [
            pltpu.make_async_copy(source.at[:, columns], target.at[:, columns], sems.at[m, n])
            for m, (source, target) in enumerate(((matrix_hbm, matrix), (features_hbm, features)))
        ]

    for n in range(chunks):
        for copy in copies(n):
            copy.start()
    total[...] = jnp.zeros_like(total)

    @pl.loop(0, chunks)
    def _(n):
        for copy in copies(n):
            copy.wait()
        columns = pl.ds(pl.multiple_of(n * width, width), width)
        total[...] += dot_nt(matrix[:, columns], features[:, columns])

    high, low = split(total[...], 2)
    sketches[:SKETCH, :] = high
    sketches[SKETCH:, :] = low
    cross_blocks(id_ref, features, sketches, (((1, 0, 0), send0), ((1, 1, 0), send1)))


def keep_kernel(id_ref, features, sketches, low0, high0, low1, high1):
    wanted = ((0, 0, 0), (0, 0, 4), (0, 1, 0), (0, 1, 4))
    cross_blocks(id_ref, features, sketches, tuple(zip(wanted, (low0, high0, low1, high1))))


def call(kernel, operands, outs, scratch=(), flops=0, limit=24, space=pltpu.VMEM):
    vmem = pl.BlockSpec(memory_space=pltpu.VMEM)
    return pl.pallas_call(
        kernel,
        out_shape=[jax.ShapeDtypeStruct(shape, dtype) for shape, dtype in outs],
        in_specs=[pl.BlockSpec(memory_space=pltpu.SMEM)]
        + [pl.BlockSpec(memory_space=space)] * (len(operands) - 1),
        out_specs=[vmem] * len(outs),
        scratch_shapes=scratch,
        compiler_params=pltpu.CompilerParams(vmem_limit_bytes=limit * 1024 * 1024),
        cost_estimate=pl.CostEstimate(flops=flops, bytes_accessed=4 * 1024 * 1024, transcendentals=0),
    )(*operands)


def scatter_stream(stream, low, high, received):
    first, second = STREAM_BITS[stream]
    back = exchange(high + received[4:], FIRST_AXIS, 1 << first)
    block = low + received[:4]
    back_next = exchange(block[2:] + back[2:], FIRST_AXIS, 1 << second)
    return block[:2] + back[:2] + back_next


def split(value, terms):
    parts = []
    for _ in range(terms):
        part = value.astype(BF16)
        parts.append(part)
        value = value - part.astype(F32)
    return parts


def dot_nt(a, b, precision=None):
    return lax.dot_general(
        a, b, (((1,), (1,)), ((), ())), precision=precision, preferred_element_type=F32
    )


def dot(a, b, precision=None):
    return jnp.dot(a, b, precision=precision, preferred_element_type=F32)


def dot_three(a, b):
    a0, a1 = split(a, 2)
    b0, b1 = split(b, 2)
    return dot(a0, b0) + (dot(a0, b1) + dot(a1, b0))


def stacked(rows, terms):
    parts = split(rows, 3)
    return jnp.concatenate([parts[n] for n in terms], axis=0)


def beside(value):
    lane = lax.broadcasted_iota(jnp.int32, value.shape, 1)
    parts = [part.astype(F32) for part in split(value, 3)]
    turned = [pltpu.roll(part, BLOCK, 1) for part in parts[:2]]
    pairs = ((0, 0), (1, 0), (2, 1))
    return jnp.concatenate(
        [jnp.where(lane < BLOCK, parts[m], turned[n]).astype(BF16) for m, n in pairs], axis=1
    )


UNDER = (0, 1, 0, 2, 0, 1)


def factor_blocks(blocks, outs, meanwhile):
    groups = BLOCK // 8
    lane = lax.broadcasted_iota(jnp.int32, (8, LANES), 1)
    sub = lax.broadcasted_iota(jnp.int32, (8, LANES), 0)
    work = []
    for block in blocks:
        rows = []
        for g in range(groups):
            unit = jnp.where(lane - BLOCK == sub + 8 * g, 1.0, 0.0).astype(F32)
            rows.append(jnp.where(lane < BLOCK, block[8 * g : 8 * g + 8], unit))
        work.append(rows)
    for g in range(groups):
        columns = [
            [
                [
                    jnp.broadcast_to(rows[r][:, 8 * g + j : 8 * g + j + 1], (8, LANES))
                    for r in range(g, groups)
                ]
                for j in range(8)
            ]
            for rows in work
        ]
        for k in range(8):
            for rows, cols, out in zip(work, columns, outs):
                pivot = cols[k][0][k : k + 1, :]
                inverse = 1.0 / pivot
                row = rows[g][k : k + 1, :]
                out[8 * g + k : 8 * g + k + 1, :] = row * lax.rsqrt(pivot)
                scaled = row * inverse
                for j in range(k + 1, 8):
                    factor = cols[j][0][k : k + 1, :] * inverse
                    for r in range(groups - g):
                        cols[j][r] = cols[j][r] - cols[k][r] * factor
                for r in range(g, groups):
                    column = cols[k][r - g]
                    if r == g:
                        column = jnp.where(sub > k, column, 0.0)
                    rows[r] = rows[r] - column * scaled
        if meanwhile:
            meanwhile.pop(0)()


def factor_all(mats, outs, upper):
    column = lax.broadcasted_iota(jnp.int32, (BLOCK, PAD), 1)
    row = lax.broadcasted_iota(jnp.int32, (BLOCK, PAD), 0)
    lane = lax.broadcasted_iota(jnp.int32, (BLOCK, LANES), 1)
    line = lax.broadcasted_iota(jnp.int32, (BLOCK, LANES), 0)
    steps = SKETCH // BLOCK
    meanwhile = []

    def update(mat, change, step, first, last):
        rows = slice(first * BLOCK, last * BLOCK)
        keep = lax.broadcasted_iota(jnp.int32, ((last - first) * BLOCK, PAD), 1)
        keep = (keep < step * BLOCK) | (keep >= (step + 1) * BLOCK)
        mat[rows, :] = jnp.where(keep, mat[rows, :], 0.0) - change

    for step in range(steps):
        here = slice(step * BLOCK, (step + 1) * BLOCK)
        window = slice(step // 2 * LANES, (step // 2 + 1) * LANES)
        odd = step % 2 == 1
        blocks = []
        for mat in mats:
            block = mat[here, window]
            blocks.append(pltpu.roll(block, BLOCK, 1) if odd else block)
        factor_blocks(blocks, outs, meanwhile)
        inside = (column >= step * BLOCK) & (column < (step + 1) * BLOCK)
        for n, (mat, out) in enumerate(zip(mats, outs)):
            both = out[...]
            inverse = beside(pltpu.roll(both, BLOCK, 1))
            line_up = jnp.where(inside, jnp.where(column - step * BLOCK == row, 1.0, 0.0), mat[here, :])
            panel = dot(inverse, stacked(line_up, UNDER))
            mat[here, :] = panel
            if n == 0:
                upper[here, :] = jnp.where(column >= (step + 1) * BLOCK, panel, 0.0)
                corner = jnp.where((lane < BLOCK) & (lane >= line), both, 0.0)
                corner = pltpu.roll(corner, BLOCK, 1) if odd else corner
                upper[here, window] = upper[here, window] + corner
            if step == steps - 1:
                continue
            start = (step + 1) * BLOCK // LANES * LANES
            turned = jnp.transpose(panel[:, start:])
            turned = jnp.concatenate([turned, jnp.zeros_like(turned)], axis=1)
            left, right = beside(turned), stacked(panel, UNDER)
            skip = (step + 1) * BLOCK - start
            update(mat, dot(left[skip : skip + BLOCK], right), step, step + 1, step + 2)
            if step < steps - 2:

                def rest(mat=mat, left=left, right=right, step=step, skip=skip):
                    stop = SKETCH - start_of(step)
                    update(mat, dot(left[skip + BLOCK : stop], right), step, step + 2, steps)

                def start_of(step):
                    return (step + 1) * BLOCK // LANES * LANES

                meanwhile.append(rest)


def columns_of(place, half, part, stream):
    role, mask = order(place, half, stream)
    first = (role << 4) | (stream << 3) | ((4 * part) ^ (mask & 4))
    return pl.ds(pl.multiple_of(first * LANES, WIDTH), WIDTH)


def pieces_kernel(member, id_ref, sketch_matrix_t, piece, *refs):
    before, (terms, sums, left, right, cross, mix) = refs[:-6], refs[-6:]
    place = coordinates(id_ref[0])
    _, mask = order(place, member[0], member[2])
    for slot in range(4):
        start = (slot ^ (mask & 2)) * LANES
        cross[:, pl.ds(pl.multiple_of(start, LANES), LANES)] = piece[slot]
    a, b, c = split(cross[...], 3)
    for n, (term, again) in enumerate(((a, a), (b, b), (c, a))):
        left[n * SKETCH : (n + 1) * SKETCH, :] = term
        terms[n * SKETCH : (n + 1) * SKETCH, :] = again
    right[:SKETCH, :] = a
    right[SKETCH:PAD, :] = jnp.zeros((PAD - SKETCH, WIDTH), BF16)
    right[PAD:, :] = sketch_matrix_t[:, columns_of(place, *member)]
    both = dot_nt(left[...], right[...])
    parts = [both[n * SKETCH : (n + 1) * SKETCH] for n in range(3)]
    mix[...] = jnp.zeros_like(mix)
    mix[:SKETCH, :SKETCH] = parts[1][:, :SKETCH] + parts[2][:, :SKETCH]
    mixed = (mix[...] + jnp.transpose(mix[...]))[:SKETCH]
    sums[...] = before[0][...] if before else jnp.zeros_like(sums)
    sums[0, :, :SKETCH] += parts[0][:, PAD:] + (parts[1][:, PAD:] + parts[2][:, PAD:])
    sums[1, :, :SKETCH] += parts[0][:, :SKETCH] + dot_nt(b, b)
    sums[1] += mixed


def factor_kernel(scale, id_ref, own, other, basis_map, inverse_c, gram, coupling, upper, out0, out1, wide):
    for n, ref in enumerate((gram, coupling)):
        ref[...] = jnp.zeros_like(ref)
        ref[:SKETCH, :] = own[n] + other[n]
    upper[...] = jnp.zeros_like(upper)
    factor_all((gram, coupling), (out0, out1), upper)
    row = lax.broadcasted_iota(jnp.int32, (PAD, PAD), 0)
    column = lax.broadcasted_iota(jnp.int32, (PAD, PAD), 1)
    lower = (row < SKETCH) & (column <= row)
    high, low = split(jnp.where(lower, gram[...], 0.0)[:SKETCH, :SKETCH], 2)
    for n, term in enumerate((high, high, low)):
        wide[:, n * SKETCH : (n + 1) * SKETCH] = term.astype(F32)
    basis_map[...] = wide[...].astype(BF16)
    chain = dot_three(jnp.where(lower, coupling[...], 0.0), jnp.transpose(upper[...]))
    gram[...] = dot_three(jnp.transpose(chain), chain) * scale
    inverse_c[...] = gram[:SKETCH, :SKETCH]


def final_kernel(members, id_ref, features, basis_map, inverse_c, *refs):
    terms, (result, coeffs) = refs[:-2], refs[-2:]
    place = coordinates(id_ref[0])
    part = WIDTH // 2

    @pl.loop(0, 2)
    def _(n):
        here = pl.ds(pl.multiple_of(n * part, part), part)
        for term, member in zip(terms, members):
            start = pl.multiple_of(columns_of(place, *member).start + n * part, part)
            coeffs[:, pl.ds(start, part)] = dot(basis_map[...], term[:, here]).astype(BF16)

    @pl.loop(0, 2)
    def _(n):
        rows = pl.ds(pl.multiple_of(n * part, part), part)
        result[:, rows] = dot_three(inverse_c[...], dot_nt(coeffs[...], features[rows, :]))


def body(features, sketch_matrix):
    rows, width = features.shape
    rows_total = rows * lax.axis_size("rows")
    device = lax.axis_index("rows").astype(jnp.int32)[None]
    whole, piece = ((8, SKETCH, LANES), F32), ((4, SKETCH, LANES), F32)
    flops = 2 * rows * width * SKETCH

    sketch_matrix_t = sketch_matrix.T

    sketches, send0, send1 = call(
        send_kernel,
        (device, features, sketch_matrix_t),
        [((2 * SKETCH, rows), BF16), whole, whole],
        scratch=[
            pltpu.VMEM((rows, width), BF16),
            pltpu.VMEM((SKETCH, width), BF16),
            pltpu.VMEM((SKETCH, rows), F32),
            pltpu.SemaphoreType.DMA((2, 4)),
        ],
        flops=2 * flops,
        space=pltpu.HBM,
        limit=50,
    )
    received = across(send0), across(send1)
    low0, high0, low1, high1 = call(
        keep_kernel, (device, features, sketches), [piece] * 4, flops=flops
    )
    block = jnp.concatenate(
        [scatter_stream(0, low0, high0, received[0]), scatter_stream(1, low1, high1, received[1])]
    )
    block = inner_sum(block, coordinates(device[0]))
    streams = []
    for stream, (first, second) in enumerate(STREAM_BITS):
        own = block[2 * stream : 2 * stream + 2]
        own = jnp.concatenate([own, exchange(own, FIRST_AXIS, 1 << second)])
        streams.append((own, exchange(own, FIRST_AXIS, 1 << first)))

    members = [(0, part, stream) for part in range(2) for stream in range(2)]
    terms_shape = ((3 * SKETCH, WIDTH), BF16)
    sums_shape = ((2, SKETCH, PAD), F32)
    terms, sums = [], ()
    for member in members:
        _, part, stream = member
        term, *sums = call(
            functools.partial(pieces_kernel, member),
            (device, sketch_matrix_t, streams[stream][part], *sums),
            [terms_shape, sums_shape],
            scratch=[
                pltpu.VMEM(*terms_shape),
                pltpu.VMEM((PAD + SKETCH, WIDTH), BF16),
                pltpu.VMEM((SKETCH, WIDTH), F32),
                pltpu.VMEM((PAD, PAD), F32),
            ],
        )
        terms.append(term)
    square, corner = pltpu.VMEM((PAD, PAD), F32), pltpu.VMEM((BLOCK, LANES), F32)
    basis_map, inverse_c = call(
        functools.partial(factor_kernel, math.sqrt(rows_total)),
        (device, *sums, across(*sums)),
        [((SKETCH, 3 * SKETCH), BF16), ((SKETCH, SKETCH), F32)],
        scratch=[square] * 3 + [corner] * 2 + [pltpu.VMEM((SKETCH, 3 * SKETCH), F32)],
        flops=14 * flops,
    )
    terms += [across(term) for term in terms]
    members += [(1, part, stream) for _, part, stream in members]
    (result,) = call(
        functools.partial(final_kernel, members),
        (device, features, basis_map, inverse_c, *terms),
        [((SKETCH, rows), F32)],
        scratch=[pltpu.VMEM((SKETCH, width), BF16)],
        flops=4 * flops,
    )
    return result.T


def solution(mesh):
    return jax.shard_map(
        body,
        mesh=mesh,
        in_specs=(P("rows", None), P()),
        out_specs=P("rows", None),
        check_vma=False,
    )
```

```python
import functools
import math

import jax
import jax.numpy as jnp
from jax import lax
from jax.experimental import pallas as pl
from jax.experimental.pallas import tpu as pltpu
from jax.sharding import PartitionSpec as P

SKETCH = 320
PAD = 384
BLOCK = 64
LANES = 128
WIDTH = 4 * LANES
F32 = jnp.float32
BF16 = jnp.bfloat16

FIRST_AXIS = ("y", "x")
SECOND_AXIS = ("x", "y")
Z_AXIS = ("z", "z")
STREAM_BITS = ((0, 1), (1, 0))


def coordinates(index):
    return {"c": index & 1, "x": (index >> 1) & 3, "z": (index >> 3) & 7, "y": (index >> 6) & 3}


def role_of(place):
    return place["c"] ^ ((place["x"] + place["y"] + place["z"]) & 1)


def gray(value):
    return value ^ (value >> 1)


def gray_of(place, role, axes):
    return jnp.where(role == 0, *(gray(place[axis]) for axis in axes))


def across(block):
    return lax.ppermute(block, "rows", [(i, i ^ 1) for i in range(lax.axis_size("rows"))])


def exchange(block, axes, bits):
    pairs = []
    for i in range(lax.axis_size("rows")):
        place = coordinates(i)
        role = role_of(place)
        wanted = gray(place[axes[role]]) ^ bits
        place[axes[role]] = next(v for v in range(8) if gray(v) == wanted)
        place["c"] ^= role ^ role_of(place)
        there = ((place["y"] * 8 + place["z"]) * 4 + place["x"]) * 2 + place["c"]
        pairs.append((i, there))
    return lax.ppermute(block, "rows", pairs)


def shifted(block, axes, shift):
    pairs = []
    for i in range(lax.axis_size("rows")):
        place = coordinates(i)
        role = role_of(place)
        place[axes[role]] = (place[axes[role]] + shift) % 4
        place["c"] ^= role ^ role_of(place)
        there = ((place["y"] * 8 + place["z"]) * 4 + place["x"]) * 2 + place["c"]
        pairs.append((i, there))
    return lax.ppermute(block, "rows", pairs)


def ring_scatter(blocks, place):
    own = jnp.where(role_of(place) == 0, *(place[axis] for axis in SECOND_AXIS))
    pick = lambda n: lax.dynamic_index_in_dim(blocks, (own + n) & 3, 0, keepdims=False)
    received = [shifted(pick(n), SECOND_AXIS, n) for n in (1, 3, 2)]
    return (pick(0) + received[0]) + (received[1] + received[2])


def ring_gather(block, place):
    own = jnp.where(role_of(place) == 0, *(place[axis] for axis in SECOND_AXIS))
    received = [(n, shifted(block, SECOND_AXIS, -n)) for n in (1, 3, 2)]
    blocks = jnp.zeros((4, *block.shape), F32)
    for n, part in [(0, block)] + received:
        blocks = lax.dynamic_update_index_in_dim(blocks, part, (own + n) & 3, 0)
    return blocks


def halve(block, place, axes, bit):
    low, high = jnp.split(block, 2)
    upper = (gray_of(place, role_of(place), axes) >> bit) & 1
    sent = exchange(jnp.where(upper == 0, high, low), axes, 1 << bit)
    return jnp.where(upper == 0, low, high) + sent


def double(block, place, axes, bit):
    upper = (gray_of(place, role_of(place), axes) >> bit) & 1
    other = exchange(block, axes, 1 << bit)
    return jnp.concatenate([jnp.where(upper == 0, block, other), jnp.where(upper == 0, other, block)])


def inner_sum(block, place):
    block = ring_scatter(block, place)
    block = halve(block, place, Z_AXIS, 0)
    others = [exchange(block, Z_AXIS, bits) for bits in (2, 4, 6)]
    block = (block + others[0]) + (others[1] + others[2])
    return ring_gather(double(block, place, Z_AXIS, 0), place)


def order(place, half, stream):
    role = role_of(place) ^ half
    code = gray_of(place, role, FIRST_AXIS)
    first, second = STREAM_BITS[stream]
    return role, (((code >> first) & 1) << 2) | (((code >> second) & 1) << 1)


def cross_blocks(id_ref, features, sketches, outs):
    place = coordinates(id_ref[0])

    @pl.loop(0, outs[0][1].shape[0] // 2)
    def _(pair):
        for (half, stream, start), out in outs:
            role, mask = order(place, half, stream)
            there = (role << 4) | (stream << 3) | ((start + 2 * pair) ^ mask)
            columns = features[:, pl.ds(pl.multiple_of(there * LANES, 256), 256)]
            both = jnp.dot(sketches[...], columns, preferred_element_type=F32)
            cross = both[:SKETCH] + both[SKETCH:]
            out[2 * pair] = cross[:, :LANES]
            out[2 * pair + 1] = cross[:, LANES:]


def send_kernel(id_ref, features_hbm, matrix_hbm, sketches, send0, send1, features, matrix, total, sems):
    chunks = sems.shape[1]
    width = features.shape[1] // chunks

    def copies(n):
        columns = pl.ds(pl.multiple_of(n * width, width), width)
        return [
            pltpu.make_async_copy(source.at[:, columns], target.at[:, columns], sems.at[m, n])
            for m, (source, target) in enumerate(((matrix_hbm, matrix), (features_hbm, features)))
        ]

    for n in range(chunks):
        for copy in copies(n):
            copy.start()
    total[...] = jnp.zeros_like(total)

    @pl.loop(0, chunks)
    def _(n):
        for copy in copies(n):
            copy.wait()
        columns = pl.ds(pl.multiple_of(n * width, width), width)
        total[...] += dot_nt(matrix[:, columns], features[:, columns])

    high, low = split(total[...], 2)
    sketches[:SKETCH, :] = high
    sketches[SKETCH:, :] = low
    cross_blocks(id_ref, features, sketches, (((1, 0, 0), send0), ((1, 1, 0), send1)))


def keep_kernel(id_ref, features, sketches, low0, high0, low1, high1):
    wanted = ((0, 0, 0), (0, 0, 4), (0, 1, 0), (0, 1, 4))
    cross_blocks(id_ref, features, sketches, tuple(zip(wanted, (low0, high0, low1, high1))))


def call(kernel, operands, outs, scratch=(), flops=0, limit=24, space=pltpu.VMEM):
    vmem = pl.BlockSpec(memory_space=pltpu.VMEM)
    return pl.pallas_call(
        kernel,
        out_shape=[jax.ShapeDtypeStruct(shape, dtype) for shape, dtype in outs],
        in_specs=[pl.BlockSpec(memory_space=pltpu.SMEM)]
        + [pl.BlockSpec(memory_space=space)] * (len(operands) - 1),
        out_specs=[vmem] * len(outs),
        scratch_shapes=scratch,
        compiler_params=pltpu.CompilerParams(vmem_limit_bytes=limit * 1024 * 1024),
        cost_estimate=pl.CostEstimate(flops=flops, bytes_accessed=4 * 1024 * 1024, transcendentals=0),
    )(*operands)


def scatter_stream(stream, low, high, received):
    first, second = STREAM_BITS[stream]
    back = exchange(high + received[4:], FIRST_AXIS, 1 << first)
    block = low + received[:4]
    back_next = exchange(block[2:] + back[2:], FIRST_AXIS, 1 << second)
    return block[:2] + back[:2] + back_next


def split(value, terms):
    parts = []
    for _ in range(terms):
        part = value.astype(BF16)
        parts.append(part)
        value = value - part.astype(F32)
    return parts


def dot_nt(a, b, precision=None):
    return lax.dot_general(
        a, b, (((1,), (1,)), ((), ())), precision=precision, preferred_element_type=F32
    )


def dot(a, b, precision=None):
    return jnp.dot(a, b, precision=precision, preferred_element_type=F32)


def dot_three(a, b):
    a0, a1 = split(a, 2)
    b0, b1 = split(b, 2)
    return dot(a0, b0) + (dot(a0, b1) + dot(a1, b0))


def stacked(rows, terms):
    parts = split(rows, 3)
    return jnp.concatenate([parts[n] for n in terms], axis=0)


def beside(value):
    lane = lax.broadcasted_iota(jnp.int32, value.shape, 1)
    parts = [part.astype(F32) for part in split(value, 3)]
    turned = [pltpu.roll(part, BLOCK, 1) for part in parts[:2]]
    pairs = ((0, 0), (1, 0), (2, 1))
    return jnp.concatenate(
        [jnp.where(lane < BLOCK, parts[m], turned[n]).astype(BF16) for m, n in pairs], axis=1
    )


UNDER = (0, 1, 0, 2, 0, 1)


def factor_blocks(blocks, outs, meanwhile):
    groups = BLOCK // 8
    lane = lax.broadcasted_iota(jnp.int32, (8, LANES), 1)
    sub = lax.broadcasted_iota(jnp.int32, (8, LANES), 0)
    work = []
    for block in blocks:
        rows = []
        for g in range(groups):
            unit = jnp.where(lane - BLOCK == sub + 8 * g, 1.0, 0.0).astype(F32)
            rows.append(jnp.where(lane < BLOCK, block[8 * g : 8 * g + 8], unit))
        work.append(rows)
    for g in range(groups):
        columns = [
            [
                [
                    jnp.broadcast_to(rows[r][:, 8 * g + j : 8 * g + j + 1], (8, LANES))
                    for r in range(g, groups)
                ]
                for j in range(8)
            ]
            for rows in work
        ]
        for k in range(8):
            for rows, cols, out in zip(work, columns, outs):
                pivot = cols[k][0][k : k + 1, :]
                inverse = 1.0 / pivot
                row = rows[g][k : k + 1, :]
                out[8 * g + k : 8 * g + k + 1, :] = row * lax.rsqrt(pivot)
                scaled = row * inverse
                for j in range(k + 1, 8):
                    factor = cols[j][0][k : k + 1, :] * inverse
                    for r in range(groups - g):
                        cols[j][r] = cols[j][r] - cols[k][r] * factor
                for r in range(g, groups):
                    column = cols[k][r - g]
                    if r == g:
                        column = jnp.where(sub > k, column, 0.0)
                    rows[r] = rows[r] - column * scaled
        if meanwhile:
            meanwhile.pop(0)()


def factor_all(mats, outs, upper):
    column = lax.broadcasted_iota(jnp.int32, (BLOCK, PAD), 1)
    row = lax.broadcasted_iota(jnp.int32, (BLOCK, PAD), 0)
    lane = lax.broadcasted_iota(jnp.int32, (BLOCK, LANES), 1)
    line = lax.broadcasted_iota(jnp.int32, (BLOCK, LANES), 0)
    steps = SKETCH // BLOCK
    meanwhile = []

    def update(mat, change, step, first, last):
        rows = slice(first * BLOCK, last * BLOCK)
        keep = lax.broadcasted_iota(jnp.int32, ((last - first) * BLOCK, PAD), 1)
        keep = (keep < step * BLOCK) | (keep >= (step + 1) * BLOCK)
        mat[rows, :] = jnp.where(keep, mat[rows, :], 0.0) - change

    for step in range(steps):
        here = slice(step * BLOCK, (step + 1) * BLOCK)
        window = slice(step // 2 * LANES, (step // 2 + 1) * LANES)
        odd = step % 2 == 1
        blocks = []
        for mat in mats:
            block = mat[here, window]
            blocks.append(pltpu.roll(block, BLOCK, 1) if odd else block)
        factor_blocks(blocks, outs, meanwhile)
        inside = (column >= step * BLOCK) & (column < (step + 1) * BLOCK)
        for n, (mat, out) in enumerate(zip(mats, outs)):
            both = out[...]
            inverse = beside(pltpu.roll(both, BLOCK, 1))
            line_up = jnp.where(inside, jnp.where(column - step * BLOCK == row, 1.0, 0.0), mat[here, :])
            panel = dot(inverse, stacked(line_up, UNDER))
            mat[here, :] = panel
            if n == 0:
                upper[here, :] = jnp.where(column >= (step + 1) * BLOCK, panel, 0.0)
                corner = jnp.where((lane < BLOCK) & (lane >= line), both, 0.0)
                corner = pltpu.roll(corner, BLOCK, 1) if odd else corner
                upper[here, window] = upper[here, window] + corner
            if step == steps - 1:
                continue
            start = (step + 1) * BLOCK // LANES * LANES
            turned = jnp.transpose(panel[:, start:])
            turned = jnp.concatenate([turned, jnp.zeros_like(turned)], axis=1)
            left, right = beside(turned), stacked(panel, UNDER)
            skip = (step + 1) * BLOCK - start
            update(mat, dot(left[skip : skip + BLOCK], right), step, step + 1, step + 2)
            if step < steps - 2:

                def rest(mat=mat, left=left, right=right, step=step, skip=skip):
                    stop = SKETCH - start_of(step)
                    update(mat, dot(left[skip + BLOCK : stop], right), step, step + 2, steps)

                def start_of(step):
                    return (step + 1) * BLOCK // LANES * LANES

                meanwhile.append(rest)


def columns_of(place, half, part, stream):
    role, mask = order(place, half, stream)
    first = (role << 4) | (stream << 3) | ((4 * part) ^ (mask & 4))
    return pl.ds(pl.multiple_of(first * LANES, WIDTH), WIDTH)


def pieces_kernel(member, id_ref, sketch_matrix_t, piece, *refs):
    before, (terms, sums, left, right, cross, mix) = refs[:-6], refs[-6:]
    place = coordinates(id_ref[0])
    _, mask = order(place, member[0], member[2])
    for slot in range(4):
        start = (slot ^ (mask & 2)) * LANES
        cross[:, pl.ds(pl.multiple_of(start, LANES), LANES)] = piece[slot]
    a, b, c = split(cross[...], 3)
    for n, (term, again) in enumerate(((a, a), (b, b), (c, a))):
        left[n * SKETCH : (n + 1) * SKETCH, :] = term
        terms[n * SKETCH : (n + 1) * SKETCH, :] = again
    right[:SKETCH, :] = a
    right[SKETCH:PAD, :] = jnp.zeros((PAD - SKETCH, WIDTH), BF16)
    right[PAD:, :] = sketch_matrix_t[:, columns_of(place, *member)]
    both = dot_nt(left[...], right[...])
    parts = [both[n * SKETCH : (n + 1) * SKETCH] for n in range(3)]
    mix[...] = jnp.zeros_like(mix)
    mix[:SKETCH, :SKETCH] = parts[1][:, :SKETCH] + parts[2][:, :SKETCH]
    mixed = (mix[...] + jnp.transpose(mix[...]))[:SKETCH]
    sums[...] = before[0][...] if before else jnp.zeros_like(sums)
    sums[0, :, :SKETCH] += parts[0][:, PAD:] + (parts[1][:, PAD:] + parts[2][:, PAD:])
    sums[1, :, :SKETCH] += parts[0][:, :SKETCH] + dot_nt(b, b)
    sums[1] += mixed


def factor_kernel(scale, id_ref, own, other, basis_map, inverse_c, gram, coupling, upper, out0, out1, wide):
    for n, ref in enumerate((gram, coupling)):
        ref[...] = jnp.zeros_like(ref)
        ref[:SKETCH, :] = own[n] + other[n]
    upper[...] = jnp.zeros_like(upper)
    factor_all((gram, coupling), (out0, out1), upper)
    row = lax.broadcasted_iota(jnp.int32, (PAD, PAD), 0)
    column = lax.broadcasted_iota(jnp.int32, (PAD, PAD), 1)
    lower = (row < SKETCH) & (column <= row)
    high, low = split(jnp.where(lower, gram[...], 0.0)[:SKETCH, :SKETCH], 2)
    for n, term in enumerate((high, high, low)):
        wide[:, n * SKETCH : (n + 1) * SKETCH] = term.astype(F32)
    basis_map[...] = wide[...].astype(BF16)
    chain = dot_three(jnp.where(lower, coupling[...], 0.0), jnp.transpose(upper[...]))
    gram[...] = dot_three(jnp.transpose(chain), chain) * scale
    inverse_c[...] = gram[:SKETCH, :SKETCH]


def final_kernel(members, id_ref, features, basis_map, inverse_c, *refs):
    terms, (result, coeffs) = refs[:-2], refs[-2:]
    place = coordinates(id_ref[0])
    part = WIDTH // 2

    @pl.loop(0, 2)
    def _(n):
        here = pl.ds(pl.multiple_of(n * part, part), part)
        for term, member in zip(terms, members):
            start = pl.multiple_of(columns_of(place, *member).start + n * part, part)
            coeffs[:, pl.ds(start, part)] = dot(basis_map[...], term[:, here]).astype(BF16)

    projected = dot_nt(coeffs[...], features[...])
    result[...] = dot_three(inverse_c[...], projected)


def body(features, sketch_matrix):
    rows, width = features.shape
    rows_total = rows * lax.axis_size("rows")
    device = lax.axis_index("rows").astype(jnp.int32)[None]
    whole, piece = ((8, SKETCH, LANES), F32), ((4, SKETCH, LANES), F32)
    flops = 2 * rows * width * SKETCH

    sketch_matrix_t = sketch_matrix.T

    sketches, send0, send1 = call(
        send_kernel,
        (device, features, sketch_matrix_t),
        [((2 * SKETCH, rows), BF16), whole, whole],
        scratch=[
            pltpu.VMEM((rows, width), BF16),
            pltpu.VMEM((SKETCH, width), BF16),
            pltpu.VMEM((SKETCH, rows), F32),
            pltpu.SemaphoreType.DMA((2, 4)),
        ],
        flops=2 * flops,
        space=pltpu.HBM,
        limit=50,
    )
    received = across(send0), across(send1)
    low0, high0, low1, high1 = call(
        keep_kernel, (device, features, sketches), [piece] * 4, flops=flops
    )
    block = jnp.concatenate(
        [scatter_stream(0, low0, high0, received[0]), scatter_stream(1, low1, high1, received[1])]
    )
    block = inner_sum(block, coordinates(device[0]))
    streams = []
    for stream, (first, second) in enumerate(STREAM_BITS):
        own = block[2 * stream : 2 * stream + 2]
        own = jnp.concatenate([own, exchange(own, FIRST_AXIS, 1 << second)])
        streams.append((own, exchange(own, FIRST_AXIS, 1 << first)))

    members = [(0, part, stream) for part in range(2) for stream in range(2)]
    terms_shape = ((3 * SKETCH, WIDTH), BF16)
    sums_shape = ((2, SKETCH, PAD), F32)
    terms, sums = [], ()
    for member in members:
        _, part, stream = member
        term, *sums = call(
            functools.partial(pieces_kernel, member),
            (device, sketch_matrix_t, streams[stream][part], *sums),
            [terms_shape, sums_shape],
            scratch=[
                pltpu.VMEM(*terms_shape),
                pltpu.VMEM((PAD + SKETCH, WIDTH), BF16),
                pltpu.VMEM((SKETCH, WIDTH), F32),
                pltpu.VMEM((PAD, PAD), F32),
            ],
        )
        terms.append(term)
    square, corner = pltpu.VMEM((PAD, PAD), F32), pltpu.VMEM((BLOCK, LANES), F32)
    basis_map, inverse_c = call(
        functools.partial(factor_kernel, math.sqrt(rows_total)),
        (device, *sums, across(*sums)),
        [((SKETCH, 3 * SKETCH), BF16), ((SKETCH, SKETCH), F32)],
        scratch=[square] * 3 + [corner] * 2 + [pltpu.VMEM((SKETCH, 3 * SKETCH), F32)],
        flops=14 * flops,
    )
    terms += [across(term) for term in terms]
    members += [(1, part, stream) for _, part, stream in members]
    (result,) = call(
        functools.partial(final_kernel, members),
        (device, features, basis_map, inverse_c, *terms),
        [((SKETCH, rows), F32)],
        scratch=[pltpu.VMEM((SKETCH, width), BF16)],
        flops=4 * flops,
    )
    return result.T


def solution(mesh):
    return jax.shard_map(
        body,
        mesh=mesh,
        in_specs=(P("rows", None), P()),
        out_specs=P("rows", None),
        check_vma=False,
    )
```

```python
import functools
import math

import jax
import jax.numpy as jnp
from jax import lax
from jax.experimental import pallas as pl
from jax.experimental.pallas import tpu as pltpu
from jax.sharding import PartitionSpec as P

SKETCH = 320
PAD = 384
BLOCK = 64
LANES = 128
WIDTH = 4 * LANES
F32 = jnp.float32
BF16 = jnp.bfloat16

FIRST_AXIS = ("y", "x")
SECOND_AXIS = ("x", "y")
Z_AXIS = ("z", "z")
STREAM_BITS = ((0, 1), (1, 0))


def coordinates(index):
    return {"c": index & 1, "x": (index >> 1) & 3, "z": (index >> 3) & 7, "y": (index >> 6) & 3}


def role_of(place):
    return place["c"] ^ ((place["x"] + place["y"] + place["z"]) & 1)


def gray(value):
    return value ^ (value >> 1)


def gray_of(place, role, axes):
    return jnp.where(role == 0, *(gray(place[axis]) for axis in axes))


def across(block):
    return lax.ppermute(block, "rows", [(i, i ^ 1) for i in range(lax.axis_size("rows"))])


def exchange(block, axes, bits):
    pairs = []
    for i in range(lax.axis_size("rows")):
        place = coordinates(i)
        role = role_of(place)
        wanted = gray(place[axes[role]]) ^ bits
        place[axes[role]] = next(v for v in range(8) if gray(v) == wanted)
        place["c"] ^= role ^ role_of(place)
        there = ((place["y"] * 8 + place["z"]) * 4 + place["x"]) * 2 + place["c"]
        pairs.append((i, there))
    return lax.ppermute(block, "rows", pairs)


def shifted(block, axes, shift):
    pairs = []
    for i in range(lax.axis_size("rows")):
        place = coordinates(i)
        role = role_of(place)
        place[axes[role]] = (place[axes[role]] + shift) % 4
        place["c"] ^= role ^ role_of(place)
        there = ((place["y"] * 8 + place["z"]) * 4 + place["x"]) * 2 + place["c"]
        pairs.append((i, there))
    return lax.ppermute(block, "rows", pairs)


def ring_scatter(blocks, place):
    own = jnp.where(role_of(place) == 0, *(place[axis] for axis in SECOND_AXIS))
    pick = lambda n: lax.dynamic_index_in_dim(blocks, (own + n) & 3, 0, keepdims=False)
    received = [shifted(pick(n), SECOND_AXIS, n) for n in (1, 3, 2)]
    return (pick(0) + received[0]) + (received[1] + received[2])


def ring_gather(block, place):
    own = jnp.where(role_of(place) == 0, *(place[axis] for axis in SECOND_AXIS))
    received = [(n, shifted(block, SECOND_AXIS, -n)) for n in (1, 3, 2)]
    blocks = jnp.zeros((4, *block.shape), F32)
    for n, part in [(0, block)] + received:
        blocks = lax.dynamic_update_index_in_dim(blocks, part, (own + n) & 3, 0)
    return blocks


def halve(block, place, axes, bit):
    low, high = jnp.split(block, 2)
    upper = (gray_of(place, role_of(place), axes) >> bit) & 1
    sent = exchange(jnp.where(upper == 0, high, low), axes, 1 << bit)
    return jnp.where(upper == 0, low, high) + sent


def double(block, place, axes, bit):
    upper = (gray_of(place, role_of(place), axes) >> bit) & 1
    other = exchange(block, axes, 1 << bit)
    return jnp.concatenate([jnp.where(upper == 0, block, other), jnp.where(upper == 0, other, block)])


def inner_sum(block, place):
    block = ring_scatter(block, place)
    block = halve(block, place, Z_AXIS, 0)
    others = [exchange(block, Z_AXIS, bits) for bits in (2, 4, 6)]
    block = (block + others[0]) + (others[1] + others[2])
    return ring_gather(double(block, place, Z_AXIS, 0), place)


def order(place, half, stream):
    role = role_of(place) ^ half
    code = gray_of(place, role, FIRST_AXIS)
    first, second = STREAM_BITS[stream]
    return role, (((code >> first) & 1) << 2) | (((code >> second) & 1) << 1)


def cross_blocks(id_ref, features, sketches, outs):
    place = coordinates(id_ref[0])

    @pl.loop(0, outs[0][1].shape[0] // 2)
    def _(pair):
        for (half, stream, start), out in outs:
            role, mask = order(place, half, stream)
            there = (role << 4) | (stream << 3) | ((start + 2 * pair) ^ mask)
            columns = features[:, pl.ds(pl.multiple_of(there * LANES, 256), 256)]
            both = jnp.dot(sketches[...], columns, preferred_element_type=F32)
            cross = both[:SKETCH] + both[SKETCH:]
            out[2 * pair] = cross[:, :LANES]
            out[2 * pair + 1] = cross[:, LANES:]


def send_kernel(id_ref, features_hbm, matrix_hbm, sketches, send0, send1, features, matrix, total, sems):
    chunks = sems.shape[1]
    width = features.shape[1] // chunks

    def copies(n):
        columns = pl.ds(pl.multiple_of(n * width, width), width)
        return [
            pltpu.make_async_copy(source.at[:, columns], target.at[:, columns], sems.at[m, n])
            for m, (source, target) in enumerate(((matrix_hbm, matrix), (features_hbm, features)))
        ]

    for n in range(chunks):
        for copy in copies(n):
            copy.start()
    total[...] = jnp.zeros_like(total)

    @pl.loop(0, chunks)
    def _(n):
        for copy in copies(n):
            copy.wait()
        columns = pl.ds(pl.multiple_of(n * width, width), width)
        total[...] += dot_nt(matrix[:, columns], features[:, columns])

    high, low = split(total[...], 2)
    sketches[:SKETCH, :] = high
    sketches[SKETCH:, :] = low
    cross_blocks(id_ref, features, sketches, (((1, 0, 0), send0), ((1, 1, 0), send1)))


def keep_kernel(id_ref, features, sketches, low0, high0, low1, high1):
    wanted = ((0, 0, 0), (0, 0, 4), (0, 1, 0), (0, 1, 4))
    cross_blocks(id_ref, features, sketches, tuple(zip(wanted, (low0, high0, low1, high1))))


def call(kernel, operands, outs, scratch=(), flops=0, limit=24, space=pltpu.VMEM):
    vmem = pl.BlockSpec(memory_space=pltpu.VMEM)
    return pl.pallas_call(
        kernel,
        out_shape=[jax.ShapeDtypeStruct(shape, dtype) for shape, dtype in outs],
        in_specs=[pl.BlockSpec(memory_space=pltpu.SMEM)]
        + [pl.BlockSpec(memory_space=space)] * (len(operands) - 1),
        out_specs=[vmem] * len(outs),
        scratch_shapes=scratch,
        compiler_params=pltpu.CompilerParams(vmem_limit_bytes=limit * 1024 * 1024),
        cost_estimate=pl.CostEstimate(flops=flops, bytes_accessed=4 * 1024 * 1024, transcendentals=0),
    )(*operands)


def scatter_stream(stream, low, high, received):
    first, second = STREAM_BITS[stream]
    back = exchange(high + received[4:], FIRST_AXIS, 1 << first)
    block = low + received[:4]
    back_next = exchange(block[2:] + back[2:], FIRST_AXIS, 1 << second)
    return block[:2] + back[:2] + back_next


def split(value, terms):
    parts = []
    for _ in range(terms):
        part = value.astype(BF16)
        parts.append(part)
        value = value - part.astype(F32)
    return parts


def dot_nt(a, b, precision=None):
    return lax.dot_general(
        a, b, (((1,), (1,)), ((), ())), precision=precision, preferred_element_type=F32
    )


def dot(a, b, precision=None):
    return jnp.dot(a, b, precision=precision, preferred_element_type=F32)


def dot_three(a, b):
    a0, a1 = split(a, 2)
    b0, b1 = split(b, 2)
    return dot(a0, b0) + (dot(a0, b1) + dot(a1, b0))


def stacked(rows, terms):
    parts = split(rows, 3)
    return jnp.concatenate([parts[n] for n in terms], axis=0)


def beside(value):
    lane = lax.broadcasted_iota(jnp.int32, value.shape, 1)
    parts = [part.astype(F32) for part in split(value, 3)]
    turned = [pltpu.roll(part, BLOCK, 1) for part in parts[:2]]
    pairs = ((0, 0), (1, 0), (2, 1))
    return jnp.concatenate(
        [jnp.where(lane < BLOCK, parts[m], turned[n]).astype(BF16) for m, n in pairs], axis=1
    )


UNDER = (0, 1, 0, 2, 0, 1)


def factor_blocks(blocks, outs, meanwhile):
    groups = BLOCK // 8
    lane = lax.broadcasted_iota(jnp.int32, (8, LANES), 1)
    sub = lax.broadcasted_iota(jnp.int32, (8, LANES), 0)
    work = []
    for block in blocks:
        rows = []
        for g in range(groups):
            unit = jnp.where(lane - BLOCK == sub + 8 * g, 1.0, 0.0).astype(F32)
            rows.append(jnp.where(lane < BLOCK, block[8 * g : 8 * g + 8], unit))
        work.append(rows)
    for g in range(groups):
        columns = [
            [
                [
                    jnp.broadcast_to(rows[r][:, 8 * g + j : 8 * g + j + 1], (8, LANES))
                    for r in range(g, groups)
                ]
                for j in range(8)
            ]
            for rows in work
        ]
        for k in range(8):
            for rows, cols, out in zip(work, columns, outs):
                pivot = cols[k][0][k : k + 1, :]
                inverse = 1.0 / pivot
                row = rows[g][k : k + 1, :]
                out[8 * g + k : 8 * g + k + 1, :] = row * lax.rsqrt(pivot)
                scaled = row * inverse
                for j in range(k + 1, 8):
                    factor = cols[j][0][k : k + 1, :] * inverse
                    for r in range(groups - g):
                        cols[j][r] = cols[j][r] - cols[k][r] * factor
                for r in range(g, groups):
                    column = cols[k][r - g]
                    if r == g:
                        column = jnp.where(sub > k, column, 0.0)
                    rows[r] = rows[r] - column * scaled
        if meanwhile:
            meanwhile.pop(0)()


def factor_all(mats, outs, upper):
    column = lax.broadcasted_iota(jnp.int32, (BLOCK, PAD), 1)
    row = lax.broadcasted_iota(jnp.int32, (BLOCK, PAD), 0)
    lane = lax.broadcasted_iota(jnp.int32, (BLOCK, LANES), 1)
    line = lax.broadcasted_iota(jnp.int32, (BLOCK, LANES), 0)
    steps = SKETCH // BLOCK
    meanwhile = []

    def update(mat, change, step, first, last):
        rows = slice(first * BLOCK, last * BLOCK)
        keep = lax.broadcasted_iota(jnp.int32, ((last - first) * BLOCK, PAD), 1)
        keep = (keep < step * BLOCK) | (keep >= (step + 1) * BLOCK)
        mat[rows, :] = jnp.where(keep, mat[rows, :], 0.0) - change

    for step in range(steps):
        here = slice(step * BLOCK, (step + 1) * BLOCK)
        window = slice(step // 2 * LANES, (step // 2 + 1) * LANES)
        odd = step % 2 == 1
        blocks = []
        for mat in mats:
            block = mat[here, window]
            blocks.append(pltpu.roll(block, BLOCK, 1) if odd else block)
        factor_blocks(blocks, outs, meanwhile)
        inside = (column >= step * BLOCK) & (column < (step + 1) * BLOCK)
        for n, (mat, out) in enumerate(zip(mats, outs)):
            both = out[...]
            inverse = beside(pltpu.roll(both, BLOCK, 1))
            line_up = jnp.where(inside, jnp.where(column - step * BLOCK == row, 1.0, 0.0), mat[here, :])
            panel = dot(inverse, stacked(line_up, UNDER))
            mat[here, :] = panel
            if n == 0:
                upper[here, :] = jnp.where(column >= (step + 1) * BLOCK, panel, 0.0)
                corner = jnp.where((lane < BLOCK) & (lane >= line), both, 0.0)
                corner = pltpu.roll(corner, BLOCK, 1) if odd else corner
                upper[here, window] = upper[here, window] + corner
            if step == steps - 1:
                continue
            start = (step + 1) * BLOCK // LANES * LANES
            turned = jnp.transpose(panel[:, start:])
            turned = jnp.concatenate([turned, jnp.zeros_like(turned)], axis=1)
            left, right = beside(turned), stacked(panel, UNDER)
            skip = (step + 1) * BLOCK - start
            update(mat, dot(left[skip : skip + BLOCK], right), step, step + 1, step + 2)
            if step < steps - 2:

                def rest(mat=mat, left=left, right=right, step=step, skip=skip):
                    stop = SKETCH - start_of(step)
                    update(mat, dot(left[skip + BLOCK : stop], right), step, step + 2, steps)

                def start_of(step):
                    return (step + 1) * BLOCK // LANES * LANES

                meanwhile.append(rest)


def columns_of(place, half, part, stream):
    role, mask = order(place, half, stream)
    first = (role << 4) | (stream << 3) | ((4 * part) ^ (mask & 4))
    return pl.ds(pl.multiple_of(first * LANES, WIDTH), WIDTH)


def pieces_kernel(member, id_ref, sketch_matrix_t, piece, *refs):
    before, (terms, sums, left, right, cross, mix) = refs[:-6], refs[-6:]
    place = coordinates(id_ref[0])
    _, mask = order(place, member[0], member[2])
    for slot in range(4):
        start = (slot ^ (mask & 2)) * LANES
        cross[:, pl.ds(pl.multiple_of(start, LANES), LANES)] = piece[slot]
    a, b, c = split(cross[...], 3)
    for n, (term, again) in enumerate(((a, a), (b, b), (c, a))):
        left[n * SKETCH : (n + 1) * SKETCH, :] = term
        terms[n * SKETCH : (n + 1) * SKETCH, :] = again
    right[:SKETCH, :] = a
    right[SKETCH:PAD, :] = jnp.zeros((PAD - SKETCH, WIDTH), BF16)
    right[PAD:, :] = sketch_matrix_t[:, columns_of(place, *member)]
    both = dot_nt(left[...], right[...])
    parts = [both[n * SKETCH : (n + 1) * SKETCH] for n in range(3)]
    mix[...] = jnp.zeros_like(mix)
    mix[:SKETCH, :SKETCH] = parts[1][:, :SKETCH] + parts[2][:, :SKETCH]
    mixed = (mix[...] + jnp.transpose(mix[...]))[:SKETCH]
    sums[...] = before[0][...] if before else jnp.zeros_like(sums)
    sums[0, :, :SKETCH] += parts[0][:, PAD:] + (parts[1][:, PAD:] + parts[2][:, PAD:])
    sums[1, :, :SKETCH] += parts[0][:, :SKETCH] + dot_nt(b, b)
    sums[1] += mixed


def factor_kernel(scale, id_ref, own, other, basis_map, inverse_c, gram, coupling, upper, out0, out1, wide):
    for n, ref in enumerate((gram, coupling)):
        ref[...] = jnp.zeros_like(ref)
        ref[:SKETCH, :] = own[n] + other[n]
    upper[...] = jnp.zeros_like(upper)
    factor_all((gram, coupling), (out0, out1), upper)
    row = lax.broadcasted_iota(jnp.int32, (PAD, PAD), 0)
    column = lax.broadcasted_iota(jnp.int32, (PAD, PAD), 1)
    lower = (row < SKETCH) & (column <= row)
    high, low = split(jnp.where(lower, gram[...], 0.0)[:SKETCH, :SKETCH], 2)
    for n, term in enumerate((high, high, low)):
        wide[:, n * SKETCH : (n + 1) * SKETCH] = term.astype(F32)
    basis_map[...] = wide[...].astype(BF16)
    chain = dot_three(jnp.where(lower, coupling[...], 0.0), jnp.transpose(upper[...]))
    gram[...] = dot_three(jnp.transpose(chain), chain) * scale
    inverse_c[...] = gram[:SKETCH, :SKETCH]


def final_kernel(members, id_ref, features, basis_map, inverse_c, *refs):
    terms, (result, coeffs) = refs[:-2], refs[-2:]
    place = coordinates(id_ref[0])
    for term, member in zip(terms, members):
        coeffs[:, columns_of(place, *member)] = dot(basis_map[...], term[...]).astype(BF16)
    projected = dot_nt(coeffs[...], features[...])
    result[...] = dot_three(inverse_c[...], projected)


def body(features, sketch_matrix):
    rows, width = features.shape
    rows_total = rows * lax.axis_size("rows")
    device = lax.axis_index("rows").astype(jnp.int32)[None]
    whole, piece = ((8, SKETCH, LANES), F32), ((4, SKETCH, LANES), F32)
    flops = 2 * rows * width * SKETCH

    sketch_matrix_t = sketch_matrix.T

    sketches, send0, send1 = call(
        send_kernel,
        (device, features, sketch_matrix_t),
        [((2 * SKETCH, rows), BF16), whole, whole],
        scratch=[
            pltpu.VMEM((rows, width), BF16),
            pltpu.VMEM((SKETCH, width), BF16),
            pltpu.VMEM((SKETCH, rows), F32),
            pltpu.SemaphoreType.DMA((2, 4)),
        ],
        flops=2 * flops,
        space=pltpu.HBM,
        limit=50,
    )
    received = across(send0), across(send1)
    low0, high0, low1, high1 = call(
        keep_kernel, (device, features, sketches), [piece] * 4, flops=flops
    )
    block = jnp.concatenate(
        [scatter_stream(0, low0, high0, received[0]), scatter_stream(1, low1, high1, received[1])]
    )
    block = inner_sum(block, coordinates(device[0]))
    streams = []
    for stream, (first, second) in enumerate(STREAM_BITS):
        own = block[2 * stream : 2 * stream + 2]
        own = jnp.concatenate([own, exchange(own, FIRST_AXIS, 1 << second)])
        streams.append((own, exchange(own, FIRST_AXIS, 1 << first)))

    members = [(0, part, stream) for part in range(2) for stream in range(2)]
    terms_shape = ((3 * SKETCH, WIDTH), BF16)
    sums_shape = ((2, SKETCH, PAD), F32)
    terms, sums = [], ()
    for member in members:
        _, part, stream = member
        term, *sums = call(
            functools.partial(pieces_kernel, member),
            (device, sketch_matrix_t, streams[stream][part], *sums),
            [terms_shape, sums_shape],
            scratch=[
                pltpu.VMEM(*terms_shape),
                pltpu.VMEM((PAD + SKETCH, WIDTH), BF16),
                pltpu.VMEM((SKETCH, WIDTH), F32),
                pltpu.VMEM((PAD, PAD), F32),
            ],
        )
        terms.append(term)
    square, corner = pltpu.VMEM((PAD, PAD), F32), pltpu.VMEM((BLOCK, LANES), F32)
    basis_map, inverse_c = call(
        functools.partial(factor_kernel, math.sqrt(rows_total)),
        (device, *sums, across(*sums)),
        [((SKETCH, 3 * SKETCH), BF16), ((SKETCH, SKETCH), F32)],
        scratch=[square] * 3 + [corner] * 2 + [pltpu.VMEM((SKETCH, 3 * SKETCH), F32)],
        flops=14 * flops,
    )
    terms += [across(term) for term in terms]
    members += [(1, part, stream) for _, part, stream in members]
    (result,) = call(
        functools.partial(final_kernel, members),
        (device, features, basis_map, inverse_c, *terms),
        [((SKETCH, rows), F32)],
        scratch=[pltpu.VMEM((SKETCH, width), BF16)],
        flops=4 * flops,
    )
    return result.T


def solution(mesh):
    return jax.shard_map(
        body,
        mesh=mesh,
        in_specs=(P("rows", None), P()),
        out_specs=P("rows", None),
        check_vma=False,
    )
```
